32 devices in a mesh: groups: 2 (over x), tensor: 16 (over z, y, core).
Axes of the slice: x: 2, y: 2, z: 4, core: 2. Of those that a mesh axis runs over, the one named last changes fastest.
Arguments:
- hidden: bfloat16 [256, 16384], P(('groups', 'tensor')), parts along dimension 0, as said below
- positions: int32 [256], P('groups'), parts along dimension 0, may hold values from 0 to 63, as said below
- norm_in: float32 [16384], replicated, may hold values from 0.1 to 1.9
- w_query: bfloat16 [16384, 2048], P(None, 'tensor'), as said below
- w_key: bfloat16 [16384, 1024], P(None, 'tensor'), as said below
- w_value: bfloat16 [16384, 1024], P(None, 'tensor'), may hold values from -0.046875 to 0.046875
- w_out: bfloat16 [2048, 16384], P('tensor'), may hold values from -0.125 to 0.125
- norm_out: float32 [16384], replicated, may hold values from 0.1 to 1.9
- w_next: bfloat16 [16384, 2048], P(None, 'tensor'), may hold values from -0.046875 to 0.046875
Outputs:
- residual_out: bfloat16 [256, 16384], P(('groups', 'tensor')), parts along dimension 0
- query_next: bfloat16 [256, 2048], P('groups', 'tensor'), parts along dimension 0
The draws below stay inside these ranges and needn't reach their ends.
There are 2 independent parts, one for each index of `groups`. The reference program is written for one: setup_inputs(seed, part) draws one part's arguments, and reference() takes and returns one part's arrays. A program takes and returns all parts, laid end to end along the dimension named above; an argument that names none is the same for every part. Nothing has to cross between parts.
Inputs may be any that keep to these rules, and one draw needn't show every extreme that they name: Within each packed document positions rise by one from 0; a document begins where the position is 0, and token 0 begins one. `w_key`: A dense random matrix of fan-in 16384. `w_query`: A dense random matrix of fan-in 16384. `hidden`: rows and features carry scales of their own.
All inputs are finite; a program needn't handle non-finite values.
Results may differ from the reference program's by a relative error of at most 0.0062.
Values may be sent and summed in bfloat16 or wider, within the bound.
A program may use at most 128 MiB of HBM per device.

```python
import math
import jax
import jax.numpy as jnp
from jax import lax

D = 16384
HD = 128
KVH = 8
HB = 128
TOKENS = 128
HEADS = 16


def shared_keys(key):
    return jax.random.normal(key, (D, KVH * HD), jnp.float32) * (1.0 / math.sqrt(D))


def draw_hidden(key, part):
    key = jax.random.fold_in(key, 1)
    value_key, row_key, column_key = jax.random.split(key, 3)
    column = jnp.arange(D).astype(jnp.float32) / D
    column_noise = jax.random.uniform(column_key, (D,), jnp.float32)
    column_scale = jnp.exp(math.log(3.0) * (column - 0.5) + math.log(2.0) * (column_noise - 0.5))
    values = jax.random.normal(value_key, (TOKENS, D), jnp.float32)
    row_scale = 0.5 * jnp.exp(math.log(10.0) * jax.random.uniform(row_key, (TOKENS, 1), jnp.float32))
    return (values * row_scale * column_scale[None, :]).astype(jnp.bfloat16)


def draw_positions(key, part):
    key = jax.random.fold_in(key, 2)
    marks = jax.random.randint(key, (TOKENS,), 0, 48)
    index = jnp.arange(TOKENS, dtype=jnp.int32)
    begins = (marks == 0) & (index >= 64) | (index % 64 == 0)
    latest = lax.cummax(jnp.where(begins, index, 0), axis=0)
    return (index - latest).astype(jnp.int32)


def draw_w_key(key, part):
    shared = shared_keys(key)
    return shared.astype(jnp.bfloat16)


def draw_w_query(key, part):
    key = jax.random.fold_in(key, 4)
    noise_key = jax.random.fold_in(key, 0)
    weight = jax.random.normal(noise_key, (D, HEADS * HD), jnp.float32) * (1.0 / math.sqrt(D))
    return weight.astype(jnp.bfloat16)


def block_levels(stream_key, dims, shards, least, high):
    def one(dim, parts):
        steps = jax.random.uniform(jax.random.fold_in(jax.random.fold_in(stream_key, 6), dim), (parts,), jnp.float32, least / len(shards), high / len(shards))
        return jnp.repeat(jnp.exp(steps), dims[dim] // parts).reshape((-1,) + (1,) * (len(dims) - dim - 1))

    factor_of = one(*shards[0])
    for cut in shards[1:]:
        factor_of = factor_of * one(*cut)
    return factor_of


def scatter_about(key, shape, spread, most, cuts=(), kind=jnp.bfloat16):
    array = spread * jax.random.normal(key, shape, jnp.float32)
    if cuts:
        array = array * block_levels(key, shape, cuts, -0.22, 0.18)
    return jnp.clip(array, -most, most).astype(kind)


def setup_inputs(seed: int = 0, part: int = 0) -> dict:
    streams_of = jax.random.split(jax.random.key(seed), 10)
    part_splits = jax.random.split(jax.random.fold_in(streams_of[9], part), 10)
    hidden = draw_hidden(jax.random.fold_in(jax.random.fold_in(streams_of[9], part), 71), part)
    positions = draw_positions(jax.random.fold_in(jax.random.fold_in(streams_of[9], part), 71), part)
    norm_in = jnp.clip(1.0 + 0.18 * jax.random.normal(streams_of[2], (D,), jnp.float32), 0.1, 1.9)
    w_query = draw_w_query(jax.random.fold_in(streams_of[9], 71), part)
    w_key = draw_w_key(jax.random.fold_in(streams_of[9], 71), part)
    w_value = scatter_about(streams_of[5], (D, KVH * HD), D ** -0.5, 0.046875, ((1, 16),))
    w_out = scatter_about(streams_of[6], (HEADS * HD, D), (HEADS * HD) ** -0.5, 0.125, ((0, 16),))
    norm_out = jnp.clip(1.0 + 0.18 * jax.random.normal(streams_of[7], (D,), jnp.float32), 0.1, 1.9)
    w_next = scatter_about(streams_of[8], (D, HEADS * HD), D ** -0.5, 0.046875, ((1, 16),))
    return dict(hidden=hidden, positions=positions, norm_in=norm_in, w_query=w_query, w_key=w_key, w_value=w_value, w_out=w_out, norm_out=norm_out, w_next=w_next)


def normalize(values, gain):
    mean_square = lax.optimization_barrier(jnp.mean(values * values, axis=-1, keepdims=True))
    return values * lax.rsqrt(mean_square + 1e-05) * gain

def rotary(values, positions, head_dim):
    count = values.shape[0]
    heads_here = values.shape[1] // head_dim
    half = head_dim // 2
    shaped = values.reshape(count, heads_here, head_dim)
    inverse = jnp.exp(-math.log(500000.0) * (2.0 * jnp.arange(half, dtype=jnp.float32) / head_dim))
    angle = positions.astype(jnp.float32)[:, None] * inverse[None, :]
    cosine = jnp.cos(angle)[:, None, :]
    sine = jnp.sin(angle)[:, None, :]
    first = shaped[:, :, :half]
    second = shaped[:, :, half:]
    turned = jnp.concatenate([first * cosine - second * sine, second * cosine + first * sine], axis=-1)
    return turned.reshape(count, heads_here * head_dim)

def attend(query, key_block, value_block, positions):
    count = positions.shape[0]
    order = jnp.arange(count, dtype=jnp.int32)
    allowed = (order[:, None] >= order[None, :]) & (positions[:, None] - positions[None, :] == order[:, None] - order[None, :])
    scores = jnp.dot(query, key_block.T, preferred_element_type=jnp.float32) * (1.0 / math.sqrt(query.shape[1]))
    scores = jnp.where(allowed, scores, -1e+30)
    largest = lax.optimization_barrier(jnp.max(scores, axis=-1, keepdims=True))
    weights = jnp.where(allowed, jnp.exp(scores - largest), 0.0)
    weights = (weights / lax.optimization_barrier(jnp.sum(weights, axis=-1, keepdims=True))).astype(jnp.bfloat16)
    return jnp.dot(weights, value_block, preferred_element_type=jnp.float32).astype(jnp.bfloat16)

def hadamard(values):
    lead = values.shape[:-1]
    width = values.shape[-1]
    blocks = width // HB
    shaped = values.reshape(lead + (blocks, HB))
    span = 1
    while span < HB:
        shaped = shaped.reshape(lead + (blocks, HB // (2 * span), 2, span))
        first = shaped[..., 0, :]
        second = shaped[..., 1, :]
        shaped = jnp.stack([first + second, first - second], axis=-2)
        span = span * 2
    return shaped.reshape(lead + (width,)) * (1.0 / math.sqrt(HB))

def head_major(values):
    count = values.shape[0]
    return jnp.transpose(values.reshape(count, HD, KVH), (0, 2, 1)).reshape(count, KVH * HD)

def reference(hidden, positions, norm_in, w_query, w_key, w_value, w_out, norm_out, w_next):
    residual = hidden.astype(jnp.float32)
    x_in = normalize(residual, norm_in).astype(jnp.bfloat16)
    queries = rotary(jnp.dot(x_in, w_query, preferred_element_type=jnp.float32), positions, HD).astype(jnp.bfloat16)
    key_raw = head_major(jnp.dot(x_in, w_key, preferred_element_type=jnp.float32).astype(jnp.bfloat16))
    value_rows = head_major(jnp.dot(x_in, w_value, preferred_element_type=jnp.float32).astype(jnp.bfloat16))
    key_rows = rotary(key_raw.astype(jnp.float32), positions, HD).astype(jnp.bfloat16)

    def one_head(total, head):
        query = lax.dynamic_slice_in_dim(queries, head * HD, HD, 1)
        group = head // (HEADS // KVH)
        key_block = lax.dynamic_slice_in_dim(key_rows, group * HD, HD, 1)
        value_block = lax.dynamic_slice_in_dim(value_rows, group * HD, HD, 1)
        context = attend(query, key_block, value_block, positions)
        out_rows = lax.dynamic_slice_in_dim(w_out, head * HD, HD, 0)
        rotated = hadamard(jnp.dot(context, out_rows, preferred_element_type=jnp.float32))
        rounded = lax.optimization_barrier(rotated.astype(jnp.bfloat16))
        return (total + rounded.astype(jnp.float32), None)
    start_total = jnp.zeros((TOKENS, D), jnp.float32)
    mixed, unused = lax.scan(one_head, start_total, jnp.arange(HEADS, dtype=jnp.int32))
    residual_f = residual + hadamard(mixed)
    residual_out = residual_f.astype(jnp.bfloat16)
    x_next = normalize(residual_f, norm_out).astype(jnp.bfloat16)
    query_next = rotary(jnp.dot(x_next, w_next, preferred_element_type=jnp.float32), positions, HD).astype(jnp.bfloat16)
    return (residual_out, query_next)
```

```python
import math

import jax
import jax.numpy as jnp
from jax import lax
from jax.experimental import pallas as pl
from jax.experimental.pallas import tpu as pltpu
from jax.sharding import PartitionSpec as P

KVH = 8
CHUNKS = 4
F32 = jnp.float32
BF16 = jnp.bfloat16


def normalize(values, gain):
    mean_square = jnp.mean(values * values, axis=-1, keepdims=True)
    return values * lax.rsqrt(mean_square + 1e-05) * gain


def rotary(values, positions, head_dim):
    count = values.shape[0]
    heads_here = values.shape[1] // head_dim
    half = head_dim // 2
    shaped = values.reshape(count, heads_here, head_dim)
    inverse = jnp.exp(-math.log(500000.0) * (2.0 * jnp.arange(half, dtype=jnp.float32) / head_dim))
    angle = positions.astype(jnp.float32)[:, None] * inverse[None, :]
    cosine = jnp.cos(angle)[:, None, :]
    sine = jnp.sin(angle)[:, None, :]
    first = shaped[:, :, :half]
    second = shaped[:, :, half:]
    turned = jnp.concatenate(
        [first * cosine - second * sine, second * cosine + first * sine], axis=-1
    )
    return turned.reshape(count, heads_here * head_dim)


def attend(query, key_block, value_block, positions):
    count = positions.shape[0]
    order = jnp.arange(count, dtype=jnp.int32)
    allowed = (order[:, None] >= order[None, :]) & (
        positions[:, None] - positions[None, :] == order[:, None] - order[None, :]
    )
    scores = jnp.dot(query, key_block.T, preferred_element_type=jnp.float32) * (
        1.0 / math.sqrt(query.shape[1])
    )
    scores = jnp.where(allowed, scores, -1e30)
    largest = jnp.max(scores, axis=-1, keepdims=True)
    weights = jnp.where(allowed, jnp.exp(scores - largest), 0.0)
    weights = (weights / jnp.sum(weights, axis=-1, keepdims=True)).astype(jnp.bfloat16)
    return jnp.dot(weights, value_block, preferred_element_type=jnp.float32).astype(jnp.bfloat16)


def block_kernel(
    hid, pos, gain_in, gain_out, wq_hbm, wk_hbm, wv_hbm, wo_hbm, wn_hbm,
    res_out, next_out,
    wq, wk, wv, wo, wn, xg1, xg2, part, rb1, s1, rb2, s2, up_out, up_in, down_out, down_in,
    kvs, kvr, acc, acc_next, squares, ctx,
    w_sem, ag_send, ag_recv, kv_send, kv_recv, sib_send, sib_recv, y_send, y_recv,
    up_send, up_recv, down_send, down_recv,
):
    me = lax.axis_index("tensor")
    c, y, z = lax.rem(me, 2), lax.rem(me // 2, 2), me // 4
    width = 16
    features = hid.shape[1]
    half = features // 2
    cw = half // CHUNKS
    tile = min(512, cw)
    tiles = cw // tile

    def index(zz, yy, cc):
        return (zz * 2 + yy) * 2 + cc

    sibling, across = index(z, y, 1 - c), index(z, 1 - y, c)
    upper, lower = index(z + 1, y, c), index(z - 1, y, c)
    pending = []

    def remote(src, dst, send, recv, device):
        return pltpu.make_async_remote_copy(
            src_ref=src, dst_ref=dst, send_sem=send, recv_sem=recv,
            device_id={"tensor": device}, device_id_type=pl.DeviceIdType.MESH,
        )

    def launch(make, when=None):
        if when is None:
            make().start()
        else:
            pl.when(when)(lambda: make().start())
        pending.append((make, when))

    weights = [
        pltpu.make_async_copy(src, dst, w_sem.at[i])
        for i, (src, dst) in enumerate(
            [(wq_hbm, wq), (wk_hbm, wk), (wv_hbm, wv), (wo_hbm, wo), (wn_hbm, wn)]
        )
    ]
    for copy in weights:
        copy.start()

    barrier = pltpu.get_barrier_semaphore()
    for step in range(1, width):
        pl.semaphore_signal(
            barrier, inc=1, device_id={"tensor": lax.rem(me + step, width)},
            device_id_type=pl.DeviceIdType.MESH,
        )

    def hidden_rows(k, off, size):
        first = hid[:, pl.ds(k * cw + off, size)].astype(F32)
        second = hid[:, pl.ds(half + k * cw + off, size)].astype(F32)
        return jnp.concatenate([first, second], axis=0)

    for k in range(CHUNKS):
        xg1[k, me] = hidden_rows(k, 0, cw).astype(BF16)
    acc[...] = jnp.zeros_like(acc)
    acc_next[...] = jnp.zeros_like(acc_next)
    squares[...] = jnp.zeros_like(squares)
    pl.semaphore_wait(barrier, width - 1)

    def gather_stages(a, xg):
        def copy(k, origin, slot, device):
            return lambda: remote(
                xg.at[k, origin], xg.at[k, origin], ag_send.at[a, k, slot], ag_recv.at[a, k, origin], device
            )

        def arrived(k, origin):
            copy(k, origin, 0, sibling)().wait_recv()

        def own(k):
            launch(copy(k, me, 0, upper), z < 3)
            launch(copy(k, me, 1, lower), z > 0)
            launch(copy(k, me, 2, across))
            launch(copy(k, me, 3, sibling))

        sides = [(d, s) for d in (1, 2, 3) for s in (0, 1)]

        def where(d, s):
            return (z - d, z >= d) if s == 0 else (z + d, z + d <= 3)

        def along(d):
            def stage(k):
                for s in (0, 1):
                    zz, there = where(d, s)
                    origin = index(zz, y, c)
                    slot = 4 + 3 * sides.index((d, s))
                    pl.when(there)(lambda: arrived(k, origin))
                    launch(copy(k, origin, slot, across), there)
                    if d < 3:
                        if s == 0:
                            launch(copy(k, origin, slot + 1, upper), there & (z < 3))
                        else:
                            launch(copy(k, origin, slot + 1, lower), there & (z > 0))
                    launch(copy(k, origin, slot + 2, sibling), there)
            return stage

        def over(d):
            def stage(k):
                if d == 0:
                    origin = index(z, 1 - y, c)
                    arrived(k, origin)
                    launch(copy(k, origin, 22, sibling))
                    return
                for s in (0, 1):
                    zz, there = where(d, s)
                    origin = index(zz, 1 - y, c)
                    pl.when(there)(lambda: arrived(k, origin))
                    launch(copy(k, origin, 23 + sides.index((d, s)), sibling), there)
            return stage

        def last(k):
            for j in range(8):
                arrived(k, j * 2 + 1 - c)

        return own, along, over, last

    def run(stages):
        for step in range(CHUNKS + max(delay for delay, _ in stages)):
            for delay, stage in stages:
                if 0 <= step - delay < CHUNKS:
                    stage(step - delay)

    def consume(xg, gain, total, load_weights, k):
        @pl.loop(0, tiles)
        def _(j):
            off = pl.multiple_of(j * tile, tile)
            block = xg[k, :, :, pl.ds(off, tile)].astype(F32)
            part_sq = squares[...]
            added = None
            for h in (0, 1):
                rows = block[:, 8 * h : 8 * h + 8, :].reshape(8 * width, tile)
                for i in range(tile // 128):
                    piece = rows[:, 128 * i : 128 * (i + 1)]
                    part_sq = part_sq + piece * piece
                at = pl.multiple_of(h * half + k * cw + off, tile)
                scaled = (rows * gain[:, pl.ds(at, tile)]).astype(BF16)
                product = jnp.dot(scaled, load_weights(pl.ds(at, tile)), preferred_element_type=F32)
                added = product if added is None else added + product
            squares[...] = part_sq
            total[...] += added

    def inverse_norm():
        mean_square = jnp.sum(squares[...], axis=1, keepdims=True) * (1.0 / features)
        return lax.rsqrt(mean_square + 1e-05)

    own, along, over, last = gather_stages(0, xg1)

    def project(k):
        if k == 0:
            for copy in weights[:3]:
                copy.wait()
        last(k)
        consume(
            xg1, gain_in, acc,
            lambda rows: jnp.concatenate([wq[rows, :], wk[rows, :], wv[rows, :]], axis=1), k,
        )

    run([(0, own), (1, along(1)), (1, over(0)), (2, along(2)), (2, over(1)), (3, along(3)),
         (3, over(2)), (4, over(3)), (5, project)])

    scale = inverse_norm()
    squares[...] = jnp.zeros_like(squares)
    raw = acc[...] * scale
    queries = raw[:, :128]
    kv = raw[:, 128:].astype(BF16)
    out_row = lax.broadcasted_iota(jnp.int32, (128, 128), 0)
    in_col = lax.broadcasted_iota(jnp.int32, (128, 128), 1)
    wanted = ((out_row // 8) % 2) * 64 + (out_row % 8) * 8 + out_row // 16
    order = jnp.where(in_col == wanted, 1.0, 0.0).astype(BF16)
    nt = (((1,), (1,)), ((), ()))
    turned = lax.dot_general(order, kv, nt, preferred_element_type=F32)
    kvs[...] = turned.astype(BF16).reshape(KVH, 16, 128)

    def kv_copy(step):
        peer = lax.rem(me + step, width)
        return lambda: remote(
            kvs.at[peer // 2], kvr.at[me], kv_send.at[step], kv_recv.at[me], peer
        )

    for step in range(1, width):
        launch(kv_copy(step))
    kvr[me] = kvs[me // 2]

    token_pos = jnp.broadcast_to(pos[...].astype(F32), (128, 128))
    exponent = lax.broadcasted_iota(jnp.int32, (64, 128), 0).astype(F32)
    inverse = jnp.exp(-math.log(500000.0) * (2.0 * exponent / 128))
    angle = token_pos[:64] * inverse
    cos_t, sin_t = jnp.cos(angle), jnp.sin(angle)
    cosine = jnp.concatenate([cos_t, cos_t], axis=0).T
    sine = jnp.concatenate([-sin_t, sin_t], axis=0).T

    def turn(values):
        return values * cosine + pltpu.roll(values, 64, 1) * sine

    query = turn(queries).astype(BF16)
    row = lax.broadcasted_iota(jnp.int32, (128, 128), 0).astype(F32)
    col = lax.broadcasted_iota(jnp.int32, (128, 128), 1).astype(F32)
    allowed = (row >= col) & (token_pos.T - token_pos == row - col)

    for step in range(1, width):
        source = lax.rem(me + step, width)
        remote(kvs.at[0], kvr.at[source], kv_send.at[step], kv_recv.at[source], sibling).wait_recv()
    both = kvr[...].astype(F32)
    key_t = both[:, 0:8, :].reshape(128, 128)
    value_t = both[:, 8:16, :].reshape(128, 128).astype(BF16)
    first, second = key_t[:64], key_t[64:]
    key_rows = jnp.concatenate(
        [first * cos_t - second * sin_t, second * cos_t + first * sin_t], axis=0
    ).astype(BF16)
    scores = jnp.dot(query, key_rows, preferred_element_type=F32) * (1.0 / math.sqrt(128))
    scores = jnp.where(allowed, scores, -1e30)
    largest = jnp.max(scores, axis=-1, keepdims=True)
    attn = jnp.where(allowed, jnp.exp(scores - largest), 0.0)
    attn = (attn / jnp.sum(attn, axis=-1, keepdims=True)).astype(BF16)
    ctx[...] = lax.dot_general(attn, value_t, nt, preferred_element_type=F32).astype(BF16)

    def tiled(body):
        @pl.loop(0, tiles)
        def _(j):
            body(pl.multiple_of(j * tile, tile))

    def multiply(k):
        if k == 0:
            weights[3].wait()

        def body(off):
            at = pl.multiple_of(k * cw + off, tile)
            one = jnp.dot(ctx[...], wo[:, pl.ds(at, tile)], preferred_element_type=F32)
            at = pl.multiple_of(half + k * cw + off, tile)
            two = jnp.dot(ctx[...], wo[:, pl.ds(at, tile)], preferred_element_type=F32)
            for t in range(width):
                rows = jnp.concatenate([one[8 * t : 8 * t + 8], two[8 * t : 8 * t + 8]], axis=0)
                part[k, t % 2, (t // 2) % 2, t // 4, :, pl.ds(off, tile)] = rows.astype(BF16)

        tiled(body)
        launch(lambda: remote(part.at[k, 1 - c], rb1.at[k], sib_send.at[k], sib_recv.at[k], sibling))

    def sum_cores(k):
        remote(part.at[k, 1 - c], rb1.at[k], sib_send.at[k], sib_recv.at[k], sibling).wait_recv()

        def body(off):
            cols = pl.ds(off, tile)
            s1[k, :, :, cols] = (
                part[k, c, 1 - y, :, :, cols].astype(F32) + rb1[k, 1 - y, :, :, cols].astype(F32)
            ).astype(BF16)

        tiled(body)
        launch(lambda: remote(s1.at[k], rb2.at[k], y_send.at[k], y_recv.at[k], across))

    def sum_across(k):
        remote(s1.at[k], rb2.at[k], y_send.at[k], y_recv.at[k], across).wait_recv()

        def body(off):
            cols = pl.ds(off, tile)
            s2[k, :, :, cols] = (
                part[k, c, y, :, :, cols].astype(F32)
                + rb1[k, y, :, :, cols].astype(F32)
                + rb2[k, :, :, cols].astype(F32)
            )

        tiled(body)

    def up_copy(k, target):
        i = target - 1
        return lambda: remote(
            up_out.at[k, i], up_in.at[k, i], up_send.at[k, i], up_recv.at[k, i], upper
        )

    def down_copy(k, target):
        return lambda: remote(
            down_out.at[k, target], down_in.at[k, target], down_send.at[k, target],
            down_recv.at[k, target], lower,
        )

    def hop(j):
        def stage(k):
            for target in (3, 2, 1):
                if target > j:
                    @pl.when(z == j)
                    def _(target=target):
                        value = s2[k, target]
                        if j > 0:
                            up_copy(k, target)().wait_recv()
                            value = value + up_in[k, target - 1].astype(F32)
                        up_out[k, target - 1] = value.astype(BF16)
                    launch(up_copy(k, target), z == j)
            for target in (0, 1, 2):
                if target < 3 - j:
                    @pl.when(z == 3 - j)
                    def _(target=target):
                        value = s2[k, target]
                        if j > 0:
                            down_copy(k, target)().wait_recv()
                            value = value + down_in[k, target].astype(F32)
                        down_out[k, target] = value.astype(BF16)
                    launch(down_copy(k, target), z == 3 - j)
        return stage

    own2, along2, over2, last2 = gather_stages(1, xg2)

    def finish(k):
        for target in range(4):
            @pl.when(z == target)
            def _(target=target):
                value = s2[k, target]
                if target > 0:
                    up_copy(k, target)().wait_recv()
                    value = value + up_in[k, target - 1].astype(F32)
                if target < 3:
                    down_copy(k, target)().wait_recv()
                    value = value + down_in[k, target].astype(F32)
                s2[k, target] = value
        residual = (s2[k, z] + hidden_rows(k, 0, cw))
        res_out[:, pl.ds(k * cw, cw)] = residual[:8].astype(BF16)
        res_out[:, pl.ds(half + k * cw, cw)] = residual[8:].astype(BF16)
        xg2[k, me] = residual.astype(BF16)
        own2(k)

    def project_next(k):
        if k == 0:
            weights[4].wait()
        last2(k)
        consume(xg2, gain_out, acc_next, lambda rows: wn[rows, :], k)

    run([(0, multiply), (1, sum_cores), (2, sum_across), (2, hop(0)), (3, hop(1)), (4, hop(2)),
         (5, finish), (6, along2(1)), (6, over2(0)), (7, along2(2)), (7, over2(1)), (8, along2(3)),
         (8, over2(2)), (9, over2(3)), (10, project_next)])

    next_out[...] = turn(acc_next[...] * inverse_norm()).astype(BF16)

    for make, when in pending:
        if when is None:
            make().wait_send()
        else:
            pl.when(when)(lambda make=make: make().wait_send())


def fused(hidden, positions, norm_in, w_query, w_key, w_value, w_out, norm_out, w_next):
    share, features = hidden.shape
    tokens = positions.shape[0]
    cw = features // 2 // CHUNKS
    columns = w_query.shape[1]
    vmem = pl.BlockSpec(memory_space=pltpu.VMEM)
    anywhere = pl.BlockSpec(memory_space=pl.ANY)
    dma = pltpu.SemaphoreType.DMA
    return pl.pallas_call(
        block_kernel,
        out_shape=(
            jax.ShapeDtypeStruct((share, features), BF16),
            jax.ShapeDtypeStruct((tokens, columns), BF16),
        ),
        in_specs=[vmem] * 4 + [anywhere] * 5,
        out_specs=(vmem, vmem),
        scratch_shapes=[
            pltpu.VMEM(w_query.shape, BF16),
            pltpu.VMEM(w_key.shape, BF16),
            pltpu.VMEM(w_value.shape, BF16),
            pltpu.VMEM(w_out.shape, BF16),
            pltpu.VMEM(w_next.shape, BF16),
            pltpu.VMEM((CHUNKS, 16, 16, cw), BF16),
            pltpu.VMEM((CHUNKS, 16, 16, cw), BF16),
            pltpu.VMEM((CHUNKS, 2, 2, 4, 16, cw), BF16),
            pltpu.VMEM((CHUNKS, 2, 4, 16, cw), BF16),
            pltpu.VMEM((CHUNKS, 4, 16, cw), BF16),
            pltpu.VMEM((CHUNKS, 4, 16, cw), BF16),
            pltpu.VMEM((CHUNKS, 4, 16, cw), F32),
            pltpu.VMEM((CHUNKS, 3, 16, cw), BF16),
            pltpu.VMEM((CHUNKS, 3, 16, cw), BF16),
            pltpu.VMEM((CHUNKS, 3, 16, cw), BF16),
            pltpu.VMEM((CHUNKS, 3, 16, cw), BF16),
            pltpu.VMEM((KVH, 16, 128), BF16),
            pltpu.VMEM((16, 16, 128), BF16),
            pltpu.VMEM((tokens, 256), F32),
            pltpu.VMEM((tokens, columns), F32),
            pltpu.VMEM((tokens, 128), F32),
            pltpu.VMEM((tokens, 128), BF16),
            dma((5,)),
            dma((2, CHUNKS, 29)),
            dma((2, CHUNKS, 16)),
            dma((16,)),
            dma((16,)),
            dma((CHUNKS,)),
            dma((CHUNKS,)),
            dma((CHUNKS,)),
            dma((CHUNKS,)),
            dma((CHUNKS, 3)),
            dma((CHUNKS, 3)),
            dma((CHUNKS, 3)),
            dma((CHUNKS, 3)),
        ],
        compiler_params=pltpu.CompilerParams(
            collective_id=0, has_side_effects=True, vmem_limit_bytes=56 * 1024 * 1024
        ),
        name="attention_block",
    )(
        hidden, positions.reshape(1, tokens), norm_in.reshape(1, features),
        norm_out.reshape(1, features), w_query, w_key, w_value, w_out, w_next,
    )


def fits(hidden, positions, w_query, w_key):
    return (
        lax.axis_size("tensor") == 16
        and hidden.shape[0] == 8
        and positions.shape[0] == 128
        and w_query.shape[1] == 128
        and w_key.shape[1] == 64
        and hidden.shape[1] % (2 * CHUNKS * 128) == 0
    )


def on_device(hidden, positions, norm_in, w_query, w_key, w_value, w_out, norm_out, w_next):
    if fits(hidden, positions, w_query, w_key):
        return fused(
            hidden, positions, norm_in, w_query, w_key, w_value, w_out, norm_out, w_next
        )
    width = lax.axis_size("tensor")
    tokens = positions.shape[0]
    share = hidden.shape[0]
    features = hidden.shape[1]
    head_dim = w_query.shape[1]
    key_cols = w_key.shape[1]
    residual = hidden.astype(jnp.float32)
    x_in = normalize(residual, norm_in).astype(jnp.bfloat16)
    w_input = jnp.concatenate([w_query, w_key, w_value], axis=1)
    projected = jnp.dot(
        lax.all_gather(x_in, "tensor", axis=0, tiled=True),
        w_input,
        preferred_element_type=jnp.float32,
    )
    queries = rotary(projected[:, :head_dim], positions, head_dim).astype(jnp.bfloat16)
    key_raw = projected[:, head_dim : head_dim + key_cols].astype(jnp.bfloat16)
    value_local = projected[:, head_dim + key_cols :].astype(jnp.bfloat16)
    local = jnp.stack([key_raw, value_local], axis=0).reshape(2, tokens, key_cols // KVH, KVH)
    per_group = jnp.transpose(local, (3, 0, 1, 2))
    sent = jnp.repeat(per_group, width // KVH, axis=0)
    pairs = lax.all_to_all(sent, "tensor", split_axis=0, concat_axis=0, tiled=True)
    pairs = jnp.transpose(pairs, (1, 2, 0, 3)).reshape(2, tokens, head_dim)
    key_block = rotary(pairs[0].astype(jnp.float32), positions, head_dim).astype(jnp.bfloat16)
    value_block = pairs[1]
    context = attend(queries, key_block, value_block, positions)
    packed = jnp.dot(context, w_out, preferred_element_type=jnp.float32).astype(jnp.bfloat16)
    received = lax.all_to_all(packed, "tensor", split_axis=0, concat_axis=0, tiled=True)
    mixed = jnp.sum(received.reshape(width, share, features).astype(jnp.float32), axis=0)
    residual_f = residual + mixed
    residual_out = residual_f.astype(jnp.bfloat16)
    x_next = normalize(residual_f, norm_out).astype(jnp.bfloat16)
    next_raw = jnp.dot(
        lax.all_gather(x_next, "tensor", axis=0, tiled=True),
        w_next,
        preferred_element_type=jnp.float32,
    )
    query_next = rotary(next_raw, positions, head_dim).astype(jnp.bfloat16)
    return (residual_out, query_next)


def solution(mesh):
    placed = (
        P(("groups", "tensor"), None),
        P("groups"),
        P(),
        P(None, "tensor"),
        P(None, "tensor"),
        P(None, "tensor"),
        P("tensor", None),
        P(),
        P(None, "tensor"),
    )
    return jax.shard_map(
        on_device,
        mesh=mesh,
        in_specs=placed,
        out_specs=(P(("groups", "tensor"), None), P("groups", "tensor")),
        check_vma=False,
    )
```

```python
import math

import jax
import jax.numpy as jnp
from jax import lax
from jax.experimental import pallas as pl
from jax.experimental.pallas import tpu as pltpu
from jax.sharding import PartitionSpec as P

KVH = 8
CHUNKS = 4
F32 = jnp.float32
BF16 = jnp.bfloat16


def normalize(values, gain):
    mean_square = jnp.mean(values * values, axis=-1, keepdims=True)
    return values * lax.rsqrt(mean_square + 1e-05) * gain


def rotary(values, positions, head_dim):
    count = values.shape[0]
    heads_here = values.shape[1] // head_dim
    half = head_dim // 2
    shaped = values.reshape(count, heads_here, head_dim)
    inverse = jnp.exp(-math.log(500000.0) * (2.0 * jnp.arange(half, dtype=jnp.float32) / head_dim))
    angle = positions.astype(jnp.float32)[:, None] * inverse[None, :]
    cosine = jnp.cos(angle)[:, None, :]
    sine = jnp.sin(angle)[:, None, :]
    first = shaped[:, :, :half]
    second = shaped[:, :, half:]
    turned = jnp.concatenate(
        [first * cosine - second * sine, second * cosine + first * sine], axis=-1
    )
    return turned.reshape(count, heads_here * head_dim)


def attend(query, key_block, value_block, positions):
    count = positions.shape[0]
    order = jnp.arange(count, dtype=jnp.int32)
    allowed = (order[:, None] >= order[None, :]) & (
        positions[:, None] - positions[None, :] == order[:, None] - order[None, :]
    )
    scores = jnp.dot(query, key_block.T, preferred_element_type=jnp.float32) * (
        1.0 / math.sqrt(query.shape[1])
    )
    scores = jnp.where(allowed, scores, -1e30)
    largest = jnp.max(scores, axis=-1, keepdims=True)
    weights = jnp.where(allowed, jnp.exp(scores - largest), 0.0)
    weights = (weights / jnp.sum(weights, axis=-1, keepdims=True)).astype(jnp.bfloat16)
    return jnp.dot(weights, value_block, preferred_element_type=jnp.float32).astype(jnp.bfloat16)


def block_kernel(
    hid, pos, gain_in, gain_out, wq_hbm, wk_hbm, wv_hbm, wo_hbm, wn_hbm,
    res_out, next_out,
    wq, wkv, wo, wn, xg1, xg2, part, rb1, s1, rb2, s2, up_out, up_in, down_out, down_in,
    kvs, kvr, acc, acc_next, squares, ctx,
    w_sem, ag_send, ag_recv, kv_send, kv_recv, sib_send, sib_recv, y_send, y_recv,
    up_send, up_recv, down_send, down_recv,
):
    me = lax.axis_index("tensor")
    c, y, z = lax.rem(me, 2), lax.rem(me // 2, 2), me // 4
    width = 16
    features = hid.shape[1]
    half = features // 2
    key_cols = wk_hbm.shape[0]
    nt = (((1,), (1,)), ((), ()))
    cw = half // CHUNKS
    tile = min(512, cw)
    tiles = cw // tile

    def index(zz, yy, cc):
        return (zz * 2 + yy) * 2 + cc

    sibling, across = index(z, y, 1 - c), index(z, 1 - y, c)
    upper, lower = index(z + 1, y, c), index(z - 1, y, c)
    pending = []

    def remote(src, dst, send, recv, device):
        return pltpu.make_async_remote_copy(
            src_ref=src, dst_ref=dst, send_sem=send, recv_sem=recv,
            device_id={"tensor": device}, device_id_type=pl.DeviceIdType.MESH,
        )

    def launch(make, when=None):
        if when is None:
            make().start()
        else:
            pl.when(when)(lambda: make().start())
        pending.append((make, when))

    weights = [
        pltpu.make_async_copy(src, dst, w_sem.at[i])
        for i, (src, dst) in enumerate(
            [(wq_hbm, wq), (wk_hbm, wkv.at[:key_cols]), (wv_hbm, wkv.at[key_cols:]), (wo_hbm, wo), (wn_hbm, wn)]
        )
    ]
    for copy in weights:
        copy.start()

    barrier = pltpu.get_barrier_semaphore()
    for step in range(1, width):
        pl.semaphore_signal(
            barrier, inc=1, device_id={"tensor": lax.rem(me + step, width)},
            device_id_type=pl.DeviceIdType.MESH,
        )

    def hidden_rows(k, off, size):
        first = hid[:, pl.ds(k * cw + off, size)].astype(F32)
        second = hid[:, pl.ds(half + k * cw + off, size)].astype(F32)
        return jnp.concatenate([first, second], axis=0)

    for k in range(CHUNKS):
        xg1[k, me] = hidden_rows(k, 0, cw).astype(BF16)
    acc[...] = jnp.zeros_like(acc)
    acc_next[...] = jnp.zeros_like(acc_next)
    squares[...] = jnp.zeros_like(squares)
    pl.semaphore_wait(barrier, width - 1)

    def gather_stages(a, xg):
        def copy(k, origin, slot, device):
            return lambda: remote(
                xg.at[k, origin], xg.at[k, origin], ag_send.at[a, k, slot], ag_recv.at[a, k, origin], device
            )

        def arrived(k, origin):
            copy(k, origin, 0, sibling)().wait_recv()

        def own(k):
            launch(copy(k, me, 0, upper), z < 3)
            launch(copy(k, me, 1, lower), z > 0)
            launch(copy(k, me, 2, across))
            launch(copy(k, me, 3, sibling))

        sides = [(d, s) for d in (1, 2, 3) for s in (0, 1)]

        def where(d, s):
            return (z - d, z >= d) if s == 0 else (z + d, z + d <= 3)

        def along(d):
            def stage(k):
                for s in (0, 1):
                    zz, there = where(d, s)
                    origin = index(zz, y, c)
                    slot = 4 + 3 * sides.index((d, s))
                    pl.when(there)(lambda: arrived(k, origin))
                    launch(copy(k, origin, slot, across), there)
                    if d < 3:
                        if s == 0:
                            launch(copy(k, origin, slot + 1, upper), there & (z < 3))
                        else:
                            launch(copy(k, origin, slot + 1, lower), there & (z > 0))
                    launch(copy(k, origin, slot + 2, sibling), there)
            return stage

        def over(d):
            def stage(k):
                if d == 0:
                    origin = index(z, 1 - y, c)
                    arrived(k, origin)
                    launch(copy(k, origin, 22, sibling))
                    return
                for s in (0, 1):
                    zz, there = where(d, s)
                    origin = index(zz, 1 - y, c)
                    pl.when(there)(lambda: arrived(k, origin))
                    launch(copy(k, origin, 23 + sides.index((d, s)), sibling), there)
            return stage

        def last(k):
            for j in range(8):
                arrived(k, j * 2 + 1 - c)

        return own, along, over, last

    def run(stages):
        for step in range(CHUNKS + max(delay for delay, _ in stages)):
            for delay, stage in stages:
                if 0 <= step - delay < CHUNKS:
                    stage(step - delay)

    def consume(xg, gain, add, k):
        @pl.loop(0, tiles)
        def _(j):
            off = pl.multiple_of(j * tile, tile)
            block = xg[k, :, :, pl.ds(off, tile)].astype(F32)
            part_sq = squares[...]
            for h in (0, 1):
                rows = block[:, 8 * h : 8 * h + 8, :].reshape(8 * width, tile)
                for i in range(tile // 128):
                    piece = rows[:, 128 * i : 128 * (i + 1)]
                    part_sq = part_sq + piece * piece
                at = pl.multiple_of(h * half + k * cw + off, tile)
                scaled = (rows * gain[:, pl.ds(at, tile)]).astype(BF16)
                add(scaled, pl.ds(at, tile))
            squares[...] = part_sq

    def inverse_norm():
        mean_square = jnp.sum(squares[...], axis=1, keepdims=True) * (1.0 / features)
        return lax.rsqrt(mean_square + 1e-05)

    own, along, over, last = gather_stages(0, xg1)

    def add_projections(scaled, at):
        acc[:, :128] += jnp.dot(scaled, wq[at, :], preferred_element_type=F32)
        acc[:, 128:] += lax.dot_general(scaled, wkv[:, at], nt, preferred_element_type=F32)

    def project(k):
        if k == 0:
            for copy in weights[:3]:
                copy.wait()
        last(k)
        consume(xg1, gain_in, add_projections, k)

    run([(0, own), (1, along(1)), (1, over(0)), (2, along(2)), (2, over(1)), (3, along(3)),
         (3, over(2)), (4, over(3)), (5, project)])

    scale = inverse_norm()
    squares[...] = jnp.zeros_like(squares)
    raw = acc[...] * scale
    queries = raw[:, :128]
    kv = raw[:, 128:].astype(BF16)
    out_row = lax.broadcasted_iota(jnp.int32, (128, 128), 0)
    in_col = lax.broadcasted_iota(jnp.int32, (128, 128), 1)
    wanted = ((out_row // 8) % 2) * 64 + (out_row % 8) * 8 + out_row // 16
    order = jnp.where(in_col == wanted, 1.0, 0.0).astype(BF16)
    turned = lax.dot_general(order, kv, nt, preferred_element_type=F32)
    kvs[...] = turned.astype(BF16).reshape(KVH, 16, 128)

    def kv_copy(step):
        peer = lax.rem(me + step, width)
        return lambda: remote(
            kvs.at[peer // 2], kvr.at[me], kv_send.at[step], kv_recv.at[me], peer
        )

    for step in range(1, width):
        launch(kv_copy(step))
    kvr[me] = kvs[me // 2]

    token_pos = jnp.broadcast_to(pos[...].astype(F32), (128, 128))
    exponent = lax.broadcasted_iota(jnp.int32, (64, 128), 0).astype(F32)
    inverse = jnp.exp(-math.log(500000.0) * (2.0 * exponent / 128))
    angle = token_pos[:64] * inverse
    cos_t, sin_t = jnp.cos(angle), jnp.sin(angle)
    cosine = jnp.concatenate([cos_t, cos_t], axis=0).T
    sine = jnp.concatenate([-sin_t, sin_t], axis=0).T

    def turn(values):
        return values * cosine + pltpu.roll(values, 64, 1) * sine

    query = turn(queries).astype(BF16)
    row = lax.broadcasted_iota(jnp.int32, (128, 128), 0).astype(F32)
    col = lax.broadcasted_iota(jnp.int32, (128, 128), 1).astype(F32)
    allowed = (row >= col) & (token_pos.T - token_pos == row - col)

    for step in range(1, width):
        source = lax.rem(me + step, width)
        remote(kvs.at[0], kvr.at[source], kv_send.at[step], kv_recv.at[source], sibling).wait_recv()
    both = kvr[...].astype(F32)
    key_t = both[:, 0:8, :].reshape(128, 128)
    value_t = both[:, 8:16, :].reshape(128, 128).astype(BF16)
    first, second = key_t[:64], key_t[64:]
    key_rows = jnp.concatenate(
        [first * cos_t - second * sin_t, second * cos_t + first * sin_t], axis=0
    ).astype(BF16)
    scores = jnp.dot(query, key_rows, preferred_element_type=F32) * (1.0 / math.sqrt(128))
    scores = jnp.where(allowed, scores, -1e30)
    largest = jnp.max(scores, axis=-1, keepdims=True)
    attn = jnp.where(allowed, jnp.exp(scores - largest), 0.0)
    attn = (attn / jnp.sum(attn, axis=-1, keepdims=True)).astype(BF16)
    ctx[...] = lax.dot_general(attn, value_t, nt, preferred_element_type=F32).astype(BF16)

    def tiled(body):
        @pl.loop(0, tiles)
        def _(j):
            body(pl.multiple_of(j * tile, tile))

    def multiply(k):
        if k == 0:
            weights[3].wait()

        def body(off):
            at = pl.multiple_of(k * cw + off, tile)
            one = jnp.dot(ctx[...], wo[:, pl.ds(at, tile)], preferred_element_type=F32)
            at = pl.multiple_of(half + k * cw + off, tile)
            two = jnp.dot(ctx[...], wo[:, pl.ds(at, tile)], preferred_element_type=F32)
            for t in range(width):
                rows = jnp.concatenate([one[8 * t : 8 * t + 8], two[8 * t : 8 * t + 8]], axis=0)
                part[k, t % 2, (t // 2) % 2, t // 4, :, pl.ds(off, tile)] = rows.astype(BF16)

        tiled(body)
        launch(lambda: remote(part.at[k, 1 - c], rb1.at[k], sib_send.at[k], sib_recv.at[k], sibling))

    def sum_cores(k):
        remote(part.at[k, 1 - c], rb1.at[k], sib_send.at[k], sib_recv.at[k], sibling).wait_recv()

        def body(off):
            cols = pl.ds(off, tile)
            s1[k, :, :, cols] = (
                part[k, c, 1 - y, :, :, cols].astype(F32) + rb1[k, 1 - y, :, :, cols].astype(F32)
            ).astype(BF16)

        tiled(body)
        launch(lambda: remote(s1.at[k], rb2.at[k], y_send.at[k], y_recv.at[k], across))

    def sum_across(k):
        remote(s1.at[k], rb2.at[k], y_send.at[k], y_recv.at[k], across).wait_recv()

        def body(off):
            cols = pl.ds(off, tile)
            s2[k, :, :, cols] = (
                part[k, c, y, :, :, cols].astype(F32)
                + rb1[k, y, :, :, cols].astype(F32)
                + rb2[k, :, :, cols].astype(F32)
            )

        tiled(body)

    def up_copy(k, target):
        i = target - 1
        return lambda: remote(
            up_out.at[k, i], up_in.at[k, i], up_send.at[k, i], up_recv.at[k, i], upper
        )

    def down_copy(k, target):
        return lambda: remote(
            down_out.at[k, target], down_in.at[k, target], down_send.at[k, target],
            down_recv.at[k, target], lower,
        )

    def hop(j):
        def stage(k):
            for target in (3, 2, 1):
                if target > j:
                    @pl.when(z == j)
                    def _(target=target):
                        value = s2[k, target]
                        if j > 0:
                            up_copy(k, target)().wait_recv()
                            value = value + up_in[k, target - 1].astype(F32)
                        up_out[k, target - 1] = value.astype(BF16)
                    launch(up_copy(k, target), z == j)
            for target in (0, 1, 2):
                if target < 3 - j:
                    @pl.when(z == 3 - j)
                    def _(target=target):
                        value = s2[k, target]
                        if j > 0:
                            down_copy(k, target)().wait_recv()
                            value = value + down_in[k, target].astype(F32)
                        down_out[k, target] = value.astype(BF16)
                    launch(down_copy(k, target), z == 3 - j)
        return stage

    own2, along2, over2, last2 = gather_stages(1, xg2)

    def finish(k):
        for target in range(4):
            @pl.when(z == target)
            def _(target=target):
                value = s2[k, target]
                if target > 0:
                    up_copy(k, target)().wait_recv()
                    value = value + up_in[k, target - 1].astype(F32)
                if target < 3:
                    down_copy(k, target)().wait_recv()
                    value = value + down_in[k, target].astype(F32)
                s2[k, target] = value
        residual = (s2[k, z] + hidden_rows(k, 0, cw))
        res_out[:, pl.ds(k * cw, cw)] = residual[:8].astype(BF16)
        res_out[:, pl.ds(half + k * cw, cw)] = residual[8:].astype(BF16)
        xg2[k, me] = residual.astype(BF16)
        own2(k)

    def add_next(scaled, at):
        acc_next[...] += jnp.dot(scaled, wn[at, :], preferred_element_type=F32)

    def project_next(k):
        if k == 0:
            weights[4].wait()
        last2(k)
        consume(xg2, gain_out, add_next, k)

    run([(0, multiply), (1, sum_cores), (2, sum_across), (2, hop(0)), (3, hop(1)), (4, hop(2)),
         (5, finish), (6, along2(1)), (6, over2(0)), (7, along2(2)), (7, over2(1)), (8, along2(3)),
         (8, over2(2)), (9, over2(3)), (10, project_next)])

    next_out[...] = turn(acc_next[...] * inverse_norm()).astype(BF16)

    for make, when in pending:
        if when is None:
            make().wait_send()
        else:
            pl.when(when)(lambda make=make: make().wait_send())


def fused(hidden, positions, norm_in, w_query, w_key, w_value, w_out, norm_out, w_next):
    share, features = hidden.shape
    tokens = positions.shape[0]
    cw = features // 2 // CHUNKS
    columns = w_query.shape[1]
    vmem = pl.BlockSpec(memory_space=pltpu.VMEM)
    anywhere = pl.BlockSpec(memory_space=pl.ANY)
    dma = pltpu.SemaphoreType.DMA
    return pl.pallas_call(
        block_kernel,
        out_shape=(
            jax.ShapeDtypeStruct((share, features), BF16),
            jax.ShapeDtypeStruct((tokens, columns), BF16),
        ),
        in_specs=[vmem] * 4 + [anywhere] * 5,
        out_specs=(vmem, vmem),
        scratch_shapes=[
            pltpu.VMEM(w_query.shape, BF16),
            pltpu.VMEM((2 * w_key.shape[1], features), BF16),
            pltpu.VMEM(w_out.shape, BF16),
            pltpu.VMEM(w_next.shape, BF16),
            pltpu.VMEM((CHUNKS, 16, 16, cw), BF16),
            pltpu.VMEM((CHUNKS, 16, 16, cw), BF16),
            pltpu.VMEM((CHUNKS, 2, 2, 4, 16, cw), BF16),
            pltpu.VMEM((CHUNKS, 2, 4, 16, cw), BF16),
            pltpu.VMEM((CHUNKS, 4, 16, cw), BF16),
            pltpu.VMEM((CHUNKS, 4, 16, cw), BF16),
            pltpu.VMEM((CHUNKS, 4, 16, cw), F32),
            pltpu.VMEM((CHUNKS, 3, 16, cw), BF16),
            pltpu.VMEM((CHUNKS, 3, 16, cw), BF16),
            pltpu.VMEM((CHUNKS, 3, 16, cw), BF16),
            pltpu.VMEM((CHUNKS, 3, 16, cw), BF16),
            pltpu.VMEM((KVH, 16, 128), BF16),
            pltpu.VMEM((16, 16, 128), BF16),
            pltpu.VMEM((tokens, 256), F32),
            pltpu.VMEM((tokens, columns), F32),
            pltpu.VMEM((tokens, 128), F32),
            pltpu.VMEM((tokens, 128), BF16),
            dma((5,)),
            dma((2, CHUNKS, 29)),
            dma((2, CHUNKS, 16)),
            dma((16,)),
            dma((16,)),
            dma((CHUNKS,)),
            dma((CHUNKS,)),
            dma((CHUNKS,)),
            dma((CHUNKS,)),
            dma((CHUNKS, 3)),
            dma((CHUNKS, 3)),
            dma((CHUNKS, 3)),
            dma((CHUNKS, 3)),
        ],
        compiler_params=pltpu.CompilerParams(
            collective_id=0, has_side_effects=True, vmem_limit_bytes=56 * 1024 * 1024
        ),
        name="attention_block",
    )(
        hidden, positions.reshape(1, tokens), norm_in.reshape(1, features),
        norm_out.reshape(1, features), w_query, w_key.T, w_value.T, w_out, w_next,
    )


def fits(hidden, positions, w_query, w_key):
    return (
        lax.axis_size("tensor") == 16
        and hidden.shape[0] == 8
        and positions.shape[0] == 128
        and w_query.shape[1] == 128
        and w_key.shape[1] == 64
        and hidden.shape[1] % (2 * CHUNKS * 128) == 0
    )


def on_device(hidden, positions, norm_in, w_query, w_key, w_value, w_out, norm_out, w_next):
    if fits(hidden, positions, w_query, w_key):
        return fused(
            hidden, positions, norm_in, w_query, w_key, w_value, w_out, norm_out, w_next
        )
    width = lax.axis_size("tensor")
    tokens = positions.shape[0]
    share = hidden.shape[0]
    features = hidden.shape[1]
    head_dim = w_query.shape[1]
    key_cols = w_key.shape[1]
    residual = hidden.astype(jnp.float32)
    x_in = normalize(residual, norm_in).astype(jnp.bfloat16)
    w_input = jnp.concatenate([w_query, w_key, w_value], axis=1)
    projected = jnp.dot(
        lax.all_gather(x_in, "tensor", axis=0, tiled=True),
        w_input,
        preferred_element_type=jnp.float32,
    )
    queries = rotary(projected[:, :head_dim], positions, head_dim).astype(jnp.bfloat16)
    key_raw = projected[:, head_dim : head_dim + key_cols].astype(jnp.bfloat16)
    value_local = projected[:, head_dim + key_cols :].astype(jnp.bfloat16)
    local = jnp.stack([key_raw, value_local], axis=0).reshape(2, tokens, key_cols // KVH, KVH)
    per_group = jnp.transpose(local, (3, 0, 1, 2))
    sent = jnp.repeat(per_group, width // KVH, axis=0)
    pairs = lax.all_to_all(sent, "tensor", split_axis=0, concat_axis=0, tiled=True)
    pairs = jnp.transpose(pairs, (1, 2, 0, 3)).reshape(2, tokens, head_dim)
    key_block = rotary(pairs[0].astype(jnp.float32), positions, head_dim).astype(jnp.bfloat16)
    value_block = pairs[1]
    context = attend(queries, key_block, value_block, positions)
    packed = jnp.dot(context, w_out, preferred_element_type=jnp.float32).astype(jnp.bfloat16)
    received = lax.all_to_all(packed, "tensor", split_axis=0, concat_axis=0, tiled=True)
    mixed = jnp.sum(received.reshape(width, share, features).astype(jnp.float32), axis=0)
    residual_f = residual + mixed
    residual_out = residual_f.astype(jnp.bfloat16)
    x_next = normalize(residual_f, norm_out).astype(jnp.bfloat16)
    next_raw = jnp.dot(
        lax.all_gather(x_next, "tensor", axis=0, tiled=True),
        w_next,
        preferred_element_type=jnp.float32,
    )
    query_next = rotary(next_raw, positions, head_dim).astype(jnp.bfloat16)
    return (residual_out, query_next)


def solution(mesh):
    placed = (
        P(("groups", "tensor"), None),
        P("groups"),
        P(),
        P(None, "tensor"),
        P(None, "tensor"),
        P(None, "tensor"),
        P("tensor", None),
        P(),
        P(None, "tensor"),
    )
    return jax.shard_map(
        on_device,
        mesh=mesh,
        in_specs=placed,
        out_specs=(P(("groups", "tensor"), None), P("groups", "tensor")),
        check_vma=False,
    )
```

```python
import math

import jax
import jax.numpy as jnp
from jax import lax
from jax.experimental import pallas as pl
from jax.experimental.pallas import tpu as pltpu
from jax.sharding import PartitionSpec as P

KVH = 8
CHUNKS = 4
F32 = jnp.float32
BF16 = jnp.bfloat16


def normalize(values, gain):
    mean_square = jnp.mean(values * values, axis=-1, keepdims=True)
    return values * lax.rsqrt(mean_square + 1e-05) * gain


def rotary(values, positions, head_dim):
    count = values.shape[0]
    heads_here = values.shape[1] // head_dim
    half = head_dim // 2
    shaped = values.reshape(count, heads_here, head_dim)
    inverse = jnp.exp(-math.log(500000.0) * (2.0 * jnp.arange(half, dtype=jnp.float32) / head_dim))
    angle = positions.astype(jnp.float32)[:, None] * inverse[None, :]
    cosine = jnp.cos(angle)[:, None, :]
    sine = jnp.sin(angle)[:, None, :]
    first = shaped[:, :, :half]
    second = shaped[:, :, half:]
    turned = jnp.concatenate(
        [first * cosine - second * sine, second * cosine + first * sine], axis=-1
    )
    return turned.reshape(count, heads_here * head_dim)


def attend(query, key_block, value_block, positions):
    count = positions.shape[0]
    order = jnp.arange(count, dtype=jnp.int32)
    allowed = (order[:, None] >= order[None, :]) & (
        positions[:, None] - positions[None, :] == order[:, None] - order[None, :]
    )
    scores = jnp.dot(query, key_block.T, preferred_element_type=jnp.float32) * (
        1.0 / math.sqrt(query.shape[1])
    )
    scores = jnp.where(allowed, scores, -1e30)
    largest = jnp.max(scores, axis=-1, keepdims=True)
    weights = jnp.where(allowed, jnp.exp(scores - largest), 0.0)
    weights = (weights / jnp.sum(weights, axis=-1, keepdims=True)).astype(jnp.bfloat16)
    return jnp.dot(weights, value_block, preferred_element_type=jnp.float32).astype(jnp.bfloat16)


def block_kernel(
    hid, pos, gain_in, gain_out, wq_hbm, wk_hbm, wv_hbm, wo_hbm, wn_hbm,
    res_out, next_out,
    wq, wkv, wo, wn, xg1, xg2, part, rb1, s1, rb2, s2, up_out, up_in, down_out, down_in,
    kvs, kvr, acc, acc_next, squares, ctx,
    w_sem, ag_send, ag_recv, sib_in, kv_send, kv_recv, sib_send, sib_recv, y_send, y_recv,
    up_send, up_recv, down_send, down_recv,
):
    me = lax.axis_index("tensor")
    c, y, z = lax.rem(me, 2), lax.rem(me // 2, 2), me // 4
    width = 16
    features = hid.shape[1]
    half = features // 2
    key_cols = wk_hbm.shape[0]
    nt = (((1,), (1,)), ((), ()))
    cw = half // CHUNKS
    tile = min(512, cw)
    tiles = cw // tile

    def index(zz, yy, cc):
        return (zz * 2 + yy) * 2 + cc

    sibling, across = index(z, y, 1 - c), index(z, 1 - y, c)
    upper, lower = index(z + 1, y, c), index(z - 1, y, c)
    pending = []

    def remote(src, dst, send, recv, device):
        return pltpu.make_async_remote_copy(
            src_ref=src, dst_ref=dst, send_sem=send, recv_sem=recv,
            device_id={"tensor": device}, device_id_type=pl.DeviceIdType.MESH,
        )

    def launch(make, when=None):
        if when is None:
            make().start()
        else:
            pl.when(when)(lambda: make().start())
        pending.append((make, when))

    weights = [
        pltpu.make_async_copy(src, dst, w_sem.at[i])
        for i, (src, dst) in enumerate(
            [(wq_hbm, wq), (wk_hbm, wkv.at[:key_cols]), (wv_hbm, wkv.at[key_cols:]), (wo_hbm, wo), (wn_hbm, wn)]
        )
    ]
    for copy in weights:
        copy.start()

    barrier = pltpu.get_barrier_semaphore()

    def greet(device):
        pl.semaphore_signal(
            barrier, inc=1, device_id={"tensor": device}, device_id_type=pl.DeviceIdType.MESH
        )

    greet(sibling)
    greet(across)
    pl.when(z < 3)(lambda: greet(upper))
    pl.when(z > 0)(lambda: greet(lower))

    def hidden_rows(k, off, size):
        first = hid[:, pl.ds(k * cw + off, size)].astype(F32)
        second = hid[:, pl.ds(half + k * cw + off, size)].astype(F32)
        return jnp.concatenate([first, second], axis=0)

    for k in range(CHUNKS):
        xg1[k, me] = hidden_rows(k, 0, cw).astype(BF16)
    acc[...] = jnp.zeros_like(acc)
    acc_next[...] = jnp.zeros_like(acc_next)
    squares[...] = jnp.zeros_like(squares)
    inner = (z > 0) & (z < 3)
    pl.when(inner)(lambda: pl.semaphore_wait(barrier, 4))
    pl.when(jnp.logical_not(inner))(lambda: pl.semaphore_wait(barrier, 3))

    def gather_stages(a, xg):
        def copy(k, origin, way, device):
            arrival = sib_in.at[a, k] if way == 3 else ag_recv.at[a, k, origin]
            return remote(
                xg.at[k, origin], xg.at[k, origin], ag_send.at[a, k, way], arrival, device
            )

        def blocks(k, count, way):
            return remote(
                xg.at[k, pl.ds(0, count)], xg.at[k, pl.ds(0, count)],
                ag_send.at[a, k, way], sib_in.at[a, k], sibling,
            )

        def arrived(k, origin):
            copy(k, origin, 0, sibling).wait_recv()

        def own(k):
            copy(k, me, 2, across).start()
            pl.when(z < 3)(lambda: copy(k, me, 0, upper).start())
            pl.when(z > 0)(lambda: copy(k, me, 1, lower).start())
            copy(k, me, 3, sibling).start()

        def along(d):
            def stage(k):
                @pl.when(z >= d)
                def _():
                    origin = index(z - d, y, c)
                    arrived(k, origin)
                    copy(k, origin, 2, across).start()
                    if d < 3:
                        pl.when(z < 3)(lambda: copy(k, origin, 0, upper).start())
                    copy(k, origin, 3, sibling).start()

                @pl.when(z + d <= 3)
                def _():
                    origin = index(z + d, y, c)
                    arrived(k, origin)
                    copy(k, origin, 2, across).start()
                    if d < 3:
                        pl.when(z > 0)(lambda: copy(k, origin, 1, lower).start())
                    copy(k, origin, 3, sibling).start()
            return stage

        def over(d):
            def pass_on(k, zz):
                origin = index(zz, 1 - y, c)
                arrived(k, origin)
                copy(k, origin, 3, sibling).start()

            def stage(k):
                if d == 0:
                    pass_on(k, z)
                else:
                    pl.when(z >= d)(lambda: pass_on(k, z - d))
                    pl.when(z + d <= 3)(lambda: pass_on(k, z + d))
            return stage

        def last(k):
            blocks(k, 8, 3).wait_recv()

        def sent(k):
            blocks(k, 4, 2).wait_send()
            blocks(k, 8, 3).wait_send()
            for at in range(4):
                @pl.when(z == at)
                def _(at=at):
                    if at < 3:
                        blocks(k, at + 1, 0).wait_send()
                    if at > 0:
                        blocks(k, 4 - at, 1).wait_send()

        return own, along, over, last, sent

    def run(stages):
        for step in range(CHUNKS + max(delay for delay, _ in stages)):
            for delay, stage in stages:
                if 0 <= step - delay < CHUNKS:
                    stage(step - delay)

    def consume(xg, gain, add, k):
        @pl.loop(0, tiles)
        def _(j):
            off = pl.multiple_of(j * tile, tile)
            block = xg[k, :, :, pl.ds(off, tile)].astype(F32)
            part_sq = squares[...]
            for h in (0, 1):
                rows = block[:, 8 * h : 8 * h + 8, :].reshape(8 * width, tile)
                for i in range(tile // 128):
                    piece = rows[:, 128 * i : 128 * (i + 1)]
                    part_sq = part_sq + piece * piece
                at = pl.multiple_of(h * half + k * cw + off, tile)
                scaled = (rows * gain[:, pl.ds(at, tile)]).astype(BF16)
                add(scaled, pl.ds(at, tile))
            squares[...] = part_sq

    def inverse_norm():
        mean_square = jnp.sum(squares[...], axis=1, keepdims=True) * (1.0 / features)
        return lax.rsqrt(mean_square + 1e-05)

    own, along, over, last, sent = gather_stages(0, xg1)

    def add_projections(scaled, at):
        acc[:, :128] += jnp.dot(scaled, wq[at, :], preferred_element_type=F32)
        acc[:, 128:] += lax.dot_general(scaled, wkv[:, at], nt, preferred_element_type=F32)

    def project(k):
        if k == 0:
            for copy in weights[:3]:
                copy.wait()
        last(k)
        consume(xg1, gain_in, add_projections, k)

    run([(0, own), (1, along(1)), (1, over(0)), (2, along(2)), (2, over(1)), (3, along(3)),
         (3, over(2)), (4, over(3)), (5, project)])

    scale = inverse_norm()
    squares[...] = jnp.zeros_like(squares)
    raw = acc[...] * scale
    queries = raw[:, :128]
    kv = raw[:, 128:].astype(BF16)
    out_row = lax.broadcasted_iota(jnp.int32, (128, 128), 0)
    in_col = lax.broadcasted_iota(jnp.int32, (128, 128), 1)
    wanted = ((out_row // 8) % 2) * 64 + (out_row % 8) * 8 + out_row // 16
    order = jnp.where(in_col == wanted, 1.0, 0.0).astype(BF16)
    turned = lax.dot_general(order, kv, nt, preferred_element_type=F32)
    kvs[...] = turned.astype(BF16).reshape(KVH, 16, 128)

    def kv_copy(step):
        peer = lax.rem(me + step, width)
        return lambda: remote(
            kvs.at[peer // 2], kvr.at[me], kv_send.at[step], kv_recv.at[me], peer
        )

    for step in range(1, width):
        launch(kv_copy(step))
    kvr[me] = kvs[me // 2]

    for k in range(CHUNKS):
        sent(k)

    token_pos = jnp.broadcast_to(pos[...].astype(F32), (128, 128))
    exponent = lax.broadcasted_iota(jnp.int32, (64, 128), 0).astype(F32)
    inverse = jnp.exp(-math.log(500000.0) * (2.0 * exponent / 128))
    angle = token_pos[:64] * inverse
    cos_t, sin_t = jnp.cos(angle), jnp.sin(angle)
    cosine = jnp.concatenate([cos_t, cos_t], axis=0).T
    sine = jnp.concatenate([-sin_t, sin_t], axis=0).T

    def turn(values):
        return values * cosine + pltpu.roll(values, 64, 1) * sine

    query = turn(queries).astype(BF16)
    row = lax.broadcasted_iota(jnp.int32, (128, 128), 0).astype(F32)
    col = lax.broadcasted_iota(jnp.int32, (128, 128), 1).astype(F32)
    allowed = (row >= col) & (token_pos.T - token_pos == row - col)

    for step in range(1, width):
        source = lax.rem(me + step, width)
        remote(kvs.at[0], kvr.at[source], kv_send.at[step], kv_recv.at[source], sibling).wait_recv()
    both = kvr[...].astype(F32)
    key_t = both[:, 0:8, :].reshape(128, 128)
    value_t = both[:, 8:16, :].reshape(128, 128).astype(BF16)
    first, second = key_t[:64], key_t[64:]
    key_rows = jnp.concatenate(
        [first * cos_t - second * sin_t, second * cos_t + first * sin_t], axis=0
    ).astype(BF16)
    scores = jnp.dot(query, key_rows, preferred_element_type=F32) * (1.0 / math.sqrt(128))
    scores = jnp.where(allowed, scores, -1e30)
    largest = jnp.max(scores, axis=-1, keepdims=True)
    attn = jnp.where(allowed, jnp.exp(scores - largest), 0.0)
    attn = (attn / jnp.sum(attn, axis=-1, keepdims=True)).astype(BF16)
    ctx[...] = lax.dot_general(attn, value_t, nt, preferred_element_type=F32).astype(BF16)

    def tiled(body):
        @pl.loop(0, tiles)
        def _(j):
            body(pl.multiple_of(j * tile, tile))

    def multiply(k):
        if k == 0:
            weights[3].wait()

        def body(off):
            at = pl.multiple_of(k * cw + off, tile)
            one = jnp.dot(ctx[...], wo[:, pl.ds(at, tile)], preferred_element_type=F32)
            at = pl.multiple_of(half + k * cw + off, tile)
            two = jnp.dot(ctx[...], wo[:, pl.ds(at, tile)], preferred_element_type=F32)
            for t in range(width):
                rows = jnp.concatenate([one[8 * t : 8 * t + 8], two[8 * t : 8 * t + 8]], axis=0)
                part[k, t % 2, (t // 2) % 2, t // 4, :, pl.ds(off, tile)] = rows.astype(BF16)

        tiled(body)
        launch(lambda: remote(part.at[k, 1 - c], rb1.at[k], sib_send.at[k], sib_recv.at[k], sibling))

    def sum_cores(k):
        remote(part.at[k, 1 - c], rb1.at[k], sib_send.at[k], sib_recv.at[k], sibling).wait_recv()

        def body(off):
            cols = pl.ds(off, tile)
            s1[k, :, :, cols] = (
                part[k, c, 1 - y, :, :, cols].astype(F32) + rb1[k, 1 - y, :, :, cols].astype(F32)
            ).astype(BF16)

        tiled(body)
        launch(lambda: remote(s1.at[k], rb2.at[k], y_send.at[k], y_recv.at[k], across))

    def sum_across(k):
        remote(s1.at[k], rb2.at[k], y_send.at[k], y_recv.at[k], across).wait_recv()

        def body(off):
            cols = pl.ds(off, tile)
            s2[k, :, :, cols] = (
                part[k, c, y, :, :, cols].astype(F32)
                + rb1[k, y, :, :, cols].astype(F32)
                + rb2[k, :, :, cols].astype(F32)
            )

        tiled(body)

    def up_copy(k, target):
        i = target - 1
        return lambda: remote(
            up_out.at[k, i], up_in.at[k, i], up_send.at[k, i], up_recv.at[k, i], upper
        )

    def down_copy(k, target):
        return lambda: remote(
            down_out.at[k, target], down_in.at[k, target], down_send.at[k, target],
            down_recv.at[k, target], lower,
        )

    def hop(j):
        def stage(k):
            for target in (3, 2, 1):
                if target > j:
                    @pl.when(z == j)
                    def _(target=target):
                        value = s2[k, target]
                        if j > 0:
                            up_copy(k, target)().wait_recv()
                            value = value + up_in[k, target - 1].astype(F32)
                        up_out[k, target - 1] = value.astype(BF16)
                        up_copy(k, target)().start()
                    pending.append((up_copy(k, target), z == j))
            for target in (0, 1, 2):
                if target < 3 - j:
                    @pl.when(z == 3 - j)
                    def _(target=target):
                        value = s2[k, target]
                        if j > 0:
                            down_copy(k, target)().wait_recv()
                            value = value + down_in[k, target].astype(F32)
                        down_out[k, target] = value.astype(BF16)
                        down_copy(k, target)().start()
                    pending.append((down_copy(k, target), z == 3 - j))
        return stage

    def drain():
        for make, when in pending:
            if when is None:
                make().wait_send()
            else:
                pl.when(when)(lambda make=make: make().wait_send())

    own2, along2, over2, last2, sent2 = gather_stages(1, xg2)

    def finish(k):
        for target in range(4):
            @pl.when(z == target)
            def _(target=target):
                value = s2[k, target]
                if target > 0:
                    up_copy(k, target)().wait_recv()
                    value = value + up_in[k, target - 1].astype(F32)
                if target < 3:
                    down_copy(k, target)().wait_recv()
                    value = value + down_in[k, target].astype(F32)
                s2[k, target] = value
        residual = (s2[k, z] + hidden_rows(k, 0, cw))
        res_out[:, pl.ds(k * cw, cw)] = residual[:8].astype(BF16)
        res_out[:, pl.ds(half + k * cw, cw)] = residual[8:].astype(BF16)
        xg2[k, me] = residual.astype(BF16)
        own2(k)

    def add_next(scaled, at):
        acc_next[...] += jnp.dot(scaled, wn[at, :], preferred_element_type=F32)

    def project_next(k):
        if k == 0:
            weights[4].wait()
        if k == CHUNKS - 1:
            drain()
        last2(k)
        consume(xg2, gain_out, add_next, k)

    run([(0, multiply), (1, sum_cores), (2, sum_across), (2, hop(0)), (3, hop(1)), (4, hop(2)),
         (5, finish), (6, along2(1)), (6, over2(0)), (7, along2(2)), (7, over2(1)), (8, along2(3)),
         (8, over2(2)), (9, over2(3)), (10, project_next)])

    next_out[...] = turn(acc_next[...] * inverse_norm()).astype(BF16)

    for k in range(CHUNKS):
        sent2(k)


def fused(hidden, positions, norm_in, w_query, w_key, w_value, w_out, norm_out, w_next):
    share, features = hidden.shape
    tokens = positions.shape[0]
    cw = features // 2 // CHUNKS
    columns = w_query.shape[1]
    vmem = pl.BlockSpec(memory_space=pltpu.VMEM)
    anywhere = pl.BlockSpec(memory_space=pl.ANY)
    dma = pltpu.SemaphoreType.DMA
    return pl.pallas_call(
        block_kernel,
        out_shape=(
            jax.ShapeDtypeStruct((share, features), BF16),
            jax.ShapeDtypeStruct((tokens, columns), BF16),
        ),
        in_specs=[vmem] * 4 + [anywhere] * 5,
        out_specs=(vmem, vmem),
        scratch_shapes=[
            pltpu.VMEM(w_query.shape, BF16),
            pltpu.VMEM((2 * w_key.shape[1], features), BF16),
            pltpu.VMEM(w_out.shape, BF16),
            pltpu.VMEM(w_next.shape, BF16),
            pltpu.VMEM((CHUNKS, 16, 16, cw), BF16),
            pltpu.VMEM((CHUNKS, 16, 16, cw), BF16),
            pltpu.VMEM((CHUNKS, 2, 2, 4, 16, cw), BF16),
            pltpu.VMEM((CHUNKS, 2, 4, 16, cw), BF16),
            pltpu.VMEM((CHUNKS, 4, 16, cw), BF16),
            pltpu.VMEM((CHUNKS, 4, 16, cw), BF16),
            pltpu.VMEM((CHUNKS, 4, 16, cw), F32),
            pltpu.VMEM((CHUNKS, 3, 16, cw), BF16),
            pltpu.VMEM((CHUNKS, 3, 16, cw), BF16),
            pltpu.VMEM((CHUNKS, 3, 16, cw), BF16),
            pltpu.VMEM((CHUNKS, 3, 16, cw), BF16),
            pltpu.VMEM((KVH, 16, 128), BF16),
            pltpu.VMEM((16, 16, 128), BF16),
            pltpu.VMEM((tokens, 256), F32),
            pltpu.VMEM((tokens, columns), F32),
            pltpu.VMEM((tokens, 128), F32),
            pltpu.VMEM((tokens, 128), BF16),
            dma((5,)),
            dma((2, CHUNKS, 4)),
            dma((2, CHUNKS, 16)),
            dma((2, CHUNKS)),
            dma((16,)),
            dma((16,)),
            dma((CHUNKS,)),
            dma((CHUNKS,)),
            dma((CHUNKS,)),
            dma((CHUNKS,)),
            dma((CHUNKS, 3)),
            dma((CHUNKS, 3)),
            dma((CHUNKS, 3)),
            dma((CHUNKS, 3)),
        ],
        compiler_params=pltpu.CompilerParams(
            collective_id=0, has_side_effects=True, vmem_limit_bytes=56 * 1024 * 1024
        ),
        name="attention_block",
    )(
        hidden, positions.reshape(1, tokens), norm_in.reshape(1, features),
        norm_out.reshape(1, features), w_query, w_key.T, w_value.T, w_out, w_next,
    )


def fits(hidden, positions, w_query, w_key):
    return (
        lax.axis_size("tensor") == 16
        and hidden.shape[0] == 8
        and positions.shape[0] == 128
        and w_query.shape[1] == 128
        and w_key.shape[1] == 64
        and hidden.shape[1] % (2 * CHUNKS * 128) == 0
    )


def on_device(hidden, positions, norm_in, w_query, w_key, w_value, w_out, norm_out, w_next):
    if fits(hidden, positions, w_query, w_key):
        return fused(
            hidden, positions, norm_in, w_query, w_key, w_value, w_out, norm_out, w_next
        )
    width = lax.axis_size("tensor")
    tokens = positions.shape[0]
    share = hidden.shape[0]
    features = hidden.shape[1]
    head_dim = w_query.shape[1]
    key_cols = w_key.shape[1]
    residual = hidden.astype(jnp.float32)
    x_in = normalize(residual, norm_in).astype(jnp.bfloat16)
    w_input = jnp.concatenate([w_query, w_key, w_value], axis=1)
    projected = jnp.dot(
        lax.all_gather(x_in, "tensor", axis=0, tiled=True),
        w_input,
        preferred_element_type=jnp.float32,
    )
    queries = rotary(projected[:, :head_dim], positions, head_dim).astype(jnp.bfloat16)
    key_raw = projected[:, head_dim : head_dim + key_cols].astype(jnp.bfloat16)
    value_local = projected[:, head_dim + key_cols :].astype(jnp.bfloat16)
    local = jnp.stack([key_raw, value_local], axis=0).reshape(2, tokens, key_cols // KVH, KVH)
    per_group = jnp.transpose(local, (3, 0, 1, 2))
    sent = jnp.repeat(per_group, width // KVH, axis=0)
    pairs = lax.all_to_all(sent, "tensor", split_axis=0, concat_axis=0, tiled=True)
    pairs = jnp.transpose(pairs, (1, 2, 0, 3)).reshape(2, tokens, head_dim)
    key_block = rotary(pairs[0].astype(jnp.float32), positions, head_dim).astype(jnp.bfloat16)
    value_block = pairs[1]
    context = attend(queries, key_block, value_block, positions)
    packed = jnp.dot(context, w_out, preferred_element_type=jnp.float32).astype(jnp.bfloat16)
    received = lax.all_to_all(packed, "tensor", split_axis=0, concat_axis=0, tiled=True)
    mixed = jnp.sum(received.reshape(width, share, features).astype(jnp.float32), axis=0)
    residual_f = residual + mixed
    residual_out = residual_f.astype(jnp.bfloat16)
    x_next = normalize(residual_f, norm_out).astype(jnp.bfloat16)
    next_raw = jnp.dot(
        lax.all_gather(x_next, "tensor", axis=0, tiled=True),
        w_next,
        preferred_element_type=jnp.float32,
    )
    query_next = rotary(next_raw, positions, head_dim).astype(jnp.bfloat16)
    return (residual_out, query_next)


def solution(mesh):
    placed = (
        P(("groups", "tensor"), None),
        P("groups"),
        P(),
        P(None, "tensor"),
        P(None, "tensor"),
        P(None, "tensor"),
        P("tensor", None),
        P(),
        P(None, "tensor"),
    )
    return jax.shard_map(
        on_device,
        mesh=mesh,
        in_specs=placed,
        out_specs=(P(("groups", "tensor"), None), P("groups", "tensor")),
        check_vma=False,
    )
```

```python
import math

import jax
import jax.numpy as jnp
from jax import lax
from jax.experimental import pallas as pl
from jax.experimental.pallas import tpu as pltpu
from jax.sharding import PartitionSpec as P

KVH = 8
CHUNKS = 8
FIRST_Y = (6,)
NEXT_Y = (7,)
SUM_Z = (0,)
ORDER_FIRST = (
    ("own", 0), ("own", 2), ("own", 7), ("own", 5), ("own", 1), ("own", 4), ("own", 3), ("own", 6),
    ("along1", 2), ("along1", 1), ("over0", 2), ("along1", 4), ("along1", 0), ("along1", 3), ("over0", 1),
    ("along2", 2), ("over0", 4), ("over0", 0), ("pre", 6), ("along2", 1), ("along2", 4), ("along2", 0),
    ("over1", 2), ("over1", 4), ("over0", 3), ("along2", 3), ("along1", 5), ("along3", 2), ("along3", 4),
    ("along1", 7), ("over1", 1), ("over1", 0), ("along1", 6), ("over2", 2), ("along3", 1), ("over1", 3),
    ("over0", 5), ("along3", 3), ("along3", 0), ("along2", 5), ("over2", 4), ("over0", 7), ("along2", 7),
    ("over3", 2), ("over2", 1), ("last", 2), ("over2", 3), ("over2", 0), ("along2", 6), ("over3", 4),
    ("over3", 3), ("over1", 5), ("over1", 7), ("along3", 5), ("over3", 0), ("along3", 7), ("last", 3),
    ("over3", 1), ("last", 0), ("last", 4), ("along3", 6), ("over2", 7), ("over2", 5), ("over3", 5),
    ("last", 1), ("over3", 7), ("last", 6), ("last", 5), ("last", 7),
)
ORDER_NEXT = (
    ("mult", 1), ("mult", 0), ("sumc", 1), ("sumc", 0), ("mult", 2), ("hop0", 0), ("sumc", 2), ("mult", 4),
    ("mult", 7), ("mult", 3), ("sumc", 3), ("suma", 1), ("hop1", 0), ("sumc", 4), ("mult", 5), ("hop0", 1),
    ("hop2", 0), ("mult", 6), ("hop1", 1), ("suma", 2), ("hop0", 2), ("suma", 3), ("hop0", 3), ("yfin", 0),
    ("hop1", 2), ("sumc", 5), ("fin", 0), ("hop1", 3), ("suma", 4), ("hop2", 1), ("own", 0), ("sumc", 6),
    ("sumc", 7), ("hop2", 2), ("hop0", 4), ("fin", 1), ("own", 1), ("hop2", 3), ("suma", 5), ("hop0", 5),
    ("hop1", 4), ("fin", 2), ("along1", 0), ("own", 2), ("hop2", 4), ("along1", 1), ("suma", 6),
    ("hop0", 6), ("over0", 0), ("hop1", 5), ("fin", 3), ("along2", 0), ("own", 3), ("suma", 7), ("hop0", 7),
    ("hop1", 6), ("hop2", 5), ("along1", 2), ("hop2", 6), ("hop1", 7), ("over1", 0), ("over0", 1),
    ("over0", 2), ("along2", 1), ("over1", 1), ("along3", 0), ("fin", 5), ("own", 5), ("fin", 4),
    ("own", 4), ("hop2", 7), ("along3", 1), ("fin", 6), ("along2", 2), ("along1", 3), ("own", 6),
    ("over0", 3), ("fin", 7), ("over2", 1), ("own", 7), ("along1", 4), ("along2", 3), ("over1", 2),
    ("along1", 5), ("over2", 0), ("along1", 6), ("over1", 3), ("over0", 4), ("along3", 2), ("over0", 5),
    ("over0", 6), ("pre", 7), ("over3", 1), ("along2", 4), ("along2", 6), ("over3", 0), ("over1", 4),
    ("along3", 3), ("over2", 3), ("last", 1), ("along2", 5), ("along1", 7), ("over2", 2), ("over1", 6),
    ("along3", 4), ("last", 0), ("over3", 2), ("over1", 5), ("along3", 6), ("along3", 5), ("along2", 7),
    ("over2", 4), ("over3", 4), ("over2", 5), ("over3", 3), ("last", 2), ("last", 4), ("over2", 6),
    ("over3", 5), ("along3", 7), ("over3", 6), ("last", 3), ("last", 5), ("last", 7), ("last", 6),
)
F32 = jnp.float32
BF16 = jnp.bfloat16


def normalize(values, gain):
    mean_square = jnp.mean(values * values, axis=-1, keepdims=True)
    return values * lax.rsqrt(mean_square + 1e-05) * gain


def rotary(values, positions, head_dim):
    count = values.shape[0]
    heads_here = values.shape[1] // head_dim
    half = head_dim // 2
    shaped = values.reshape(count, heads_here, head_dim)
    inverse = jnp.exp(-math.log(500000.0) * (2.0 * jnp.arange(half, dtype=jnp.float32) / head_dim))
    angle = positions.astype(jnp.float32)[:, None] * inverse[None, :]
    cosine = jnp.cos(angle)[:, None, :]
    sine = jnp.sin(angle)[:, None, :]
    first = shaped[:, :, :half]
    second = shaped[:, :, half:]
    turned = jnp.concatenate(
        [first * cosine - second * sine, second * cosine + first * sine], axis=-1
    )
    return turned.reshape(count, heads_here * head_dim)


def attend(query, key_block, value_block, positions):
    count = positions.shape[0]
    order = jnp.arange(count, dtype=jnp.int32)
    allowed = (order[:, None] >= order[None, :]) & (
        positions[:, None] - positions[None, :] == order[:, None] - order[None, :]
    )
    scores = jnp.dot(query, key_block.T, preferred_element_type=jnp.float32) * (
        1.0 / math.sqrt(query.shape[1])
    )
    scores = jnp.where(allowed, scores, -1e30)
    largest = jnp.max(scores, axis=-1, keepdims=True)
    weights = jnp.where(allowed, jnp.exp(scores - largest), 0.0)
    weights = (weights / jnp.sum(weights, axis=-1, keepdims=True)).astype(jnp.bfloat16)
    return jnp.dot(weights, value_block, preferred_element_type=jnp.float32).astype(jnp.bfloat16)


def block_kernel(
    hid, pos, gain_in, gain_out, wq_hbm, wk_hbm, wv_hbm, wo_hbm, wn_hbm,
    res_out, next_out,
    wq, wkv, wo, wn, xg1, xg2, part, rb1, s1, rb2, s2, up_out, up_in, down_out, down_in,
    kvs, kvr, acc, acc_next, squares, ctx,
    w_sem, ag_send, ag_recv, sib_in, kv_send, kv_recv, sib_send, sib_recv, y_send, y_recv,
    up_send, up_recv, down_send, down_recv,
):
    me = lax.axis_index("tensor")
    c, y, z = lax.rem(me, 2), lax.rem(me // 2, 2), me // 4
    width = 16
    features = hid.shape[1]
    half = features // 2
    key_cols = wk_hbm.shape[0]
    nt = (((1,), (1,)), ((), ()))
    cw = half // CHUNKS
    tile = min(512, cw)
    tiles = cw // tile

    def index(zz, yy, cc):
        return (zz * 2 + yy) * 2 + cc

    sibling, across = index(z, y, 1 - c), index(z, 1 - y, c)
    upper, lower = index(z + 1, y, c), index(z - 1, y, c)
    pending = []

    def remote(src, dst, send, recv, device):
        return pltpu.make_async_remote_copy(
            src_ref=src, dst_ref=dst, send_sem=send, recv_sem=recv,
            device_id={"tensor": device}, device_id_type=pl.DeviceIdType.MESH,
        )

    def launch(make, when=None):
        if when is None:
            make().start()
        else:
            pl.when(when)(lambda: make().start())
        pending.append((make, when))

    weights = [
        pltpu.make_async_copy(src, dst, w_sem.at[i])
        for i, (src, dst) in enumerate(
            [(wq_hbm, wq), (wk_hbm, wkv.at[:key_cols]), (wv_hbm, wkv.at[key_cols:]), (wo_hbm, wo), (wn_hbm, wn)]
        )
    ]
    for copy in weights:
        copy.start()

    barrier = pltpu.get_barrier_semaphore()

    def greet(device):
        pl.semaphore_signal(
            barrier, inc=1, device_id={"tensor": device}, device_id_type=pl.DeviceIdType.MESH
        )

    greet(sibling)
    greet(across)
    pl.when(z < 3)(lambda: greet(upper))
    pl.when(z > 0)(lambda: greet(lower))

    def hidden_rows(k, off, size):
        first = hid[:, pl.ds(k * cw + off, size)].astype(F32)
        second = hid[:, pl.ds(half + k * cw + off, size)].astype(F32)
        return jnp.concatenate([first, second], axis=0)

    for k in range(CHUNKS):
        xg1[k, me] = hidden_rows(k, 0, cw).astype(BF16)
    acc[...] = jnp.zeros_like(acc)
    acc_next[...] = jnp.zeros_like(acc_next)
    squares[...] = jnp.zeros_like(squares)
    inner = (z > 0) & (z < 3)
    pl.when(inner)(lambda: pl.semaphore_wait(barrier, 4))
    pl.when(jnp.logical_not(inner))(lambda: pl.semaphore_wait(barrier, 3))

    def gather_stages(a, xg, y_first):
        def copy(k, origin, way, device):
            arrival = sib_in.at[a, k] if way == 3 else ag_recv.at[a, k, origin]
            return remote(
                xg.at[k, origin], xg.at[k, origin], ag_send.at[a, k, way], arrival, device
            )

        def blocks(k, count, way):
            return remote(
                xg.at[k, pl.ds(0, count)], xg.at[k, pl.ds(0, count)],
                ag_send.at[a, k, way], sib_in.at[a, k], sibling,
            )

        def arrived(k, origin):
            copy(k, origin, 0, sibling).wait_recv()

        def own(k):
            copy(k, me, 2, across).start()
            pl.when(z < 3)(lambda: copy(k, me, 0, upper).start())
            pl.when(z > 0)(lambda: copy(k, me, 1, lower).start())
            copy(k, me, 3, sibling).start()

        def early(k):
            if k in y_first:
                origin = index(z, 1 - y, c)
                arrived(k, origin)
                pl.when(z < 3)(lambda: copy(k, origin, 0, upper).start())
                pl.when(z > 0)(lambda: copy(k, origin, 1, lower).start())
                copy(k, origin, 3, sibling).start()

        def along(d):
            def both(k):
                for yy in (y, 1 - y):
                    @pl.when(z >= d)
                    def _(origin=index(z - d, yy, c)):
                        arrived(k, origin)
                        if d < 3:
                            pl.when(z < 3)(lambda: copy(k, origin, 0, upper).start())
                        copy(k, origin, 3, sibling).start()

                    @pl.when(z + d <= 3)
                    def _(origin=index(z + d, yy, c)):
                        arrived(k, origin)
                        if d < 3:
                            pl.when(z > 0)(lambda: copy(k, origin, 1, lower).start())
                        copy(k, origin, 3, sibling).start()

            def stage(k):
                if k in y_first:
                    both(k)
                    return

                @pl.when(z >= d)
                def _():
                    origin = index(z - d, y, c)
                    arrived(k, origin)
                    copy(k, origin, 2, across).start()
                    if d < 3:
                        pl.when(z < 3)(lambda: copy(k, origin, 0, upper).start())
                    copy(k, origin, 3, sibling).start()

                @pl.when(z + d <= 3)
                def _():
                    origin = index(z + d, y, c)
                    arrived(k, origin)
                    copy(k, origin, 2, across).start()
                    if d < 3:
                        pl.when(z > 0)(lambda: copy(k, origin, 1, lower).start())
                    copy(k, origin, 3, sibling).start()
            return stage

        def over(d):
            def pass_on(k, zz):
                origin = index(zz, 1 - y, c)
                arrived(k, origin)
                copy(k, origin, 3, sibling).start()

            def stage(k):
                if k in y_first:
                    return
                if d == 0:
                    pass_on(k, z)
                else:
                    pl.when(z >= d)(lambda: pass_on(k, z - d))
                    pl.when(z + d <= 3)(lambda: pass_on(k, z + d))
            return stage

        def last(k):
            blocks(k, 8, 3).wait_recv()

        def sent(k):
            spread = 2 if k in y_first else 1
            blocks(k, 1 if k in y_first else 4, 2).wait_send()
            blocks(k, 8, 3).wait_send()
            for at in range(4):
                @pl.when(z == at)
                def _(at=at):
                    if at < 3:
                        blocks(k, spread * (at + 1), 0).wait_send()
                    if at > 0:
                        blocks(k, spread * (4 - at), 1).wait_send()

        return own, early, along, over, last, sent

    def run(stages, order):
        for name, k in order:
            stages[name](k)

    def consume(xg, gain, add, k):
        @pl.loop(0, tiles)
        def _(j):
            off = pl.multiple_of(j * tile, tile)
            block = xg[k, :, :, pl.ds(off, tile)].astype(F32)
            part_sq = squares[...]
            for h in (0, 1):
                rows = block[:, 8 * h : 8 * h + 8, :].reshape(8 * width, tile)
                for i in range(tile // 128):
                    piece = rows[:, 128 * i : 128 * (i + 1)]
                    part_sq = part_sq + piece * piece
                at = pl.multiple_of(h * half + k * cw + off, tile)
                scaled = (rows * gain[:, pl.ds(at, tile)]).astype(BF16)
                add(scaled, pl.ds(at, tile))
            squares[...] = part_sq

    def inverse_norm():
        mean_square = jnp.sum(squares[...], axis=1, keepdims=True) * (1.0 / features)
        return lax.rsqrt(mean_square + 1e-05)

    own, early, along, over, last, sent = gather_stages(0, xg1, FIRST_Y)

    def add_projections(scaled, at):
        acc[:, :128] += jnp.dot(scaled, wq[at, :], preferred_element_type=F32)
        acc[:, 128:] += lax.dot_general(scaled, wkv[:, at], nt, preferred_element_type=F32)

    first_used = [k for name, k in ORDER_FIRST if name == "last"][0]

    def project(k):
        if k == first_used:
            for copy in weights[:3]:
                copy.wait()
        last(k)
        consume(xg1, gain_in, add_projections, k)

    run(dict(own=own, pre=early, along1=along(1), along2=along(2), along3=along(3), over0=over(0),
             over1=over(1), over2=over(2), over3=over(3), last=project), ORDER_FIRST)

    scale = inverse_norm()
    squares[...] = jnp.zeros_like(squares)
    raw = acc[...] * scale
    queries = raw[:, :128]
    kv = raw[:, 128:].astype(BF16)
    out_row = lax.broadcasted_iota(jnp.int32, (128, 128), 0)
    in_col = lax.broadcasted_iota(jnp.int32, (128, 128), 1)
    wanted = ((out_row // 8) % 2) * 64 + (out_row % 8) * 8 + out_row // 16
    order = jnp.where(in_col == wanted, 1.0, 0.0).astype(BF16)
    turned = lax.dot_general(order, kv, nt, preferred_element_type=F32)
    kvs[...] = turned.astype(BF16).reshape(KVH, 16, 128)

    def kv_copy(step):
        peer = lax.rem(me + step, width)
        return lambda: remote(
            kvs.at[peer // 2], kvr.at[me], kv_send.at[step], kv_recv.at[me], peer
        )

    for step in range(1, width):
        launch(kv_copy(step))
    kvr[me] = kvs[me // 2]

    for k in range(CHUNKS):
        sent(k)

    token_pos = jnp.broadcast_to(pos[...].astype(F32), (128, 128))
    exponent = lax.broadcasted_iota(jnp.int32, (64, 128), 0).astype(F32)
    inverse = jnp.exp(-math.log(500000.0) * (2.0 * exponent / 128))
    angle = token_pos[:64] * inverse
    cos_t, sin_t = jnp.cos(angle), jnp.sin(angle)
    cosine = jnp.concatenate([cos_t, cos_t], axis=0).T
    sine = jnp.concatenate([-sin_t, sin_t], axis=0).T

    def turn(values):
        return values * cosine + pltpu.roll(values, 64, 1) * sine

    query = turn(queries).astype(BF16)
    row = lax.broadcasted_iota(jnp.int32, (128, 128), 0).astype(F32)
    col = lax.broadcasted_iota(jnp.int32, (128, 128), 1).astype(F32)
    allowed = (row >= col) & (token_pos.T - token_pos == row - col)

    for step in range(1, width):
        source = lax.rem(me + step, width)
        remote(kvs.at[0], kvr.at[source], kv_send.at[step], kv_recv.at[source], sibling).wait_recv()
    both = kvr[...].astype(F32)
    key_t = both[:, 0:8, :].reshape(128, 128)
    value_t = both[:, 8:16, :].reshape(128, 128).astype(BF16)
    first, second = key_t[:64], key_t[64:]
    key_rows = jnp.concatenate(
        [first * cos_t - second * sin_t, second * cos_t + first * sin_t], axis=0
    ).astype(BF16)
    scores = jnp.dot(query, key_rows, preferred_element_type=F32) * (1.0 / math.sqrt(128))
    scores = jnp.where(allowed, scores, -1e30)
    largest = jnp.max(scores, axis=-1, keepdims=True)
    attn = jnp.where(allowed, jnp.exp(scores - largest), 0.0)
    attn = (attn / jnp.sum(attn, axis=-1, keepdims=True)).astype(BF16)
    ctx[...] = lax.dot_general(attn, value_t, nt, preferred_element_type=F32).astype(BF16)

    def tiled(body):
        @pl.loop(0, tiles)
        def _(j):
            body(pl.multiple_of(j * tile, tile))

    def multiply(k):
        if k == ORDER_NEXT[0][1]:
            weights[3].wait()

        def body(off):
            at = pl.multiple_of(k * cw + off, tile)
            one = jnp.dot(ctx[...], wo[:, pl.ds(at, tile)], preferred_element_type=F32)
            at = pl.multiple_of(half + k * cw + off, tile)
            two = jnp.dot(ctx[...], wo[:, pl.ds(at, tile)], preferred_element_type=F32)
            for t in range(width):
                rows = jnp.concatenate([one[8 * t : 8 * t + 8], two[8 * t : 8 * t + 8]], axis=0)
                part[k, t % 2, (t // 2) % 2, t // 4, :, pl.ds(off, tile)] = rows.astype(BF16)

        tiled(body)
        launch(lambda: remote(part.at[k, 1 - c], rb1.at[k], sib_send.at[k], sib_recv.at[k], sibling))

    def sum_cores(k):
        remote(part.at[k, 1 - c], rb1.at[k], sib_send.at[k], sib_recv.at[k], sibling).wait_recv()

        def body(off):
            cols = pl.ds(off, tile)
            theirs = (
                part[k, c, 1 - y, :, :, cols].astype(F32) + rb1[k, 1 - y, :, :, cols].astype(F32)
            )
            if k in SUM_Z:
                s2[1, k, :, :, cols] = theirs
                s2[0, k, :, :, cols] = (
                    part[k, c, y, :, :, cols].astype(F32) + rb1[k, y, :, :, cols].astype(F32)
                )
            else:
                s1[k, :, :, cols] = theirs.astype(BF16)

        tiled(body)
        if k in SUM_Z:
            return
        launch(lambda: remote(s1.at[k], rb2.at[k], y_send.at[k], y_recv.at[k], across))

    def sum_across(k):
        if k in SUM_Z:
            return
        remote(s1.at[k], rb2.at[k], y_send.at[k], y_recv.at[k], across).wait_recv()

        def body(off):
            cols = pl.ds(off, tile)
            s2[0, k, :, :, cols] = (
                part[k, c, y, :, :, cols].astype(F32)
                + rb1[k, y, :, :, cols].astype(F32)
                + rb2[k, :, :, cols].astype(F32)
            )

        tiled(body)

    def up_copy(k, o, target):
        i = target - 1
        return lambda: remote(
            up_out.at[k, o, i], up_in.at[k, o, i], up_send.at[k, o, i], up_recv.at[k, o, i], upper
        )

    def down_copy(k, o, target):
        return lambda: remote(
            down_out.at[k, o, target], down_in.at[k, o, target], down_send.at[k, o, target],
            down_recv.at[k, o, target], lower,
        )

    def hop(j):
        def stage(k):
            for o in (0, 1) if k in SUM_Z else (0,):
                @pl.when(z == j)
                def _(o=o):
                    for target in range(3, j, -1):
                        value = s2[o, k, target]
                        if j > 0:
                            up_copy(k, o, target)().wait_recv()
                            value = value + up_in[k, o, target - 1].astype(F32)
                        up_out[k, o, target - 1] = value.astype(BF16)
                        up_copy(k, o, target)().start()

                @pl.when(z == 3 - j)
                def _(o=o):
                    for target in range(3 - j):
                        value = s2[o, k, target]
                        if j > 0:
                            down_copy(k, o, target)().wait_recv()
                            value = value + down_in[k, o, target].astype(F32)
                        down_out[k, o, target] = value.astype(BF16)
                        down_copy(k, o, target)().start()

                for target in range(3, j, -1):
                    pending.append((up_copy(k, o, target), z == j))
                for target in range(3 - j):
                    pending.append((down_copy(k, o, target), z == 3 - j))
        return stage

    def whole_line(k, o, then):
        for target in range(4):
            @pl.when(z == target)
            def _(target=target):
                value = s2[o, k, target]
                if target > 0:
                    up_copy(k, o, target)().wait_recv()
                    value = value + up_in[k, o, target - 1].astype(F32)
                if target < 3:
                    down_copy(k, o, target)().wait_recv()
                    value = value + down_in[k, o, target].astype(F32)
                then(value)

    def across_copy(k):
        return lambda: remote(s1.at[k, 0], rb2.at[k, 0], y_send.at[k], y_recv.at[k], across)

    def hand_across(k):
        if k in SUM_Z:
            def keep(value):
                s1[k, 0] = value.astype(BF16)
            whole_line(k, 1, keep)
            launch(across_copy(k))

    def drain():
        for make, when in pending:
            if when is None:
                make().wait_send()
            else:
                pl.when(when)(lambda make=make: make().wait_send())

    own2, early2, along2, over2, last2, sent2 = gather_stages(1, xg2, NEXT_Y)

    def finish(k):
        def keep(value):
            s2[0, k, 0] = value
        whole_line(k, 0, keep)
        mixed = s2[0, k, 0]
        if k in SUM_Z:
            across_copy(k)().wait_recv()
            mixed = mixed + rb2[k, 0].astype(F32)
        residual = mixed + hidden_rows(k, 0, cw)
        res_out[:, pl.ds(k * cw, cw)] = residual[:8].astype(BF16)
        res_out[:, pl.ds(half + k * cw, cw)] = residual[8:].astype(BF16)
        xg2[k, me] = residual.astype(BF16)

    def add_next(scaled, at):
        acc_next[...] += jnp.dot(scaled, wn[at, :], preferred_element_type=F32)

    next_used = [k for name, k in ORDER_NEXT if name == "last"][0]

    def project_next(k):
        if k == next_used:
            weights[4].wait()
        if k == ORDER_NEXT[-1][1]:
            drain()
        last2(k)
        consume(xg2, gain_out, add_next, k)

    run(dict(mult=multiply, sumc=sum_cores, suma=sum_across, hop0=hop(0), hop1=hop(1), hop2=hop(2),
             yfin=hand_across, fin=finish, own=own2, pre=early2, along1=along2(1), along2=along2(2),
             along3=along2(3), over0=over2(0), over1=over2(1), over2=over2(2), over3=over2(3),
             last=project_next), ORDER_NEXT)

    next_out[...] = turn(acc_next[...] * inverse_norm()).astype(BF16)

    for k in range(CHUNKS):
        sent2(k)


def fused(hidden, positions, norm_in, w_query, w_key, w_value, w_out, norm_out, w_next):
    share, features = hidden.shape
    tokens = positions.shape[0]
    cw = features // 2 // CHUNKS
    columns = w_query.shape[1]
    vmem = pl.BlockSpec(memory_space=pltpu.VMEM)
    anywhere = pl.BlockSpec(memory_space=pl.ANY)
    dma = pltpu.SemaphoreType.DMA
    return pl.pallas_call(
        block_kernel,
        out_shape=(
            jax.ShapeDtypeStruct((share, features), BF16),
            jax.ShapeDtypeStruct((tokens, columns), BF16),
        ),
        in_specs=[vmem] * 4 + [anywhere] * 5,
        out_specs=(vmem, vmem),
        scratch_shapes=[
            pltpu.VMEM(w_query.shape, BF16),
            pltpu.VMEM((2 * w_key.shape[1], features), BF16),
            pltpu.VMEM(w_out.shape, BF16),
            pltpu.VMEM(w_next.shape, BF16),
            pltpu.VMEM((CHUNKS, 16, 16, cw), BF16),
            pltpu.VMEM((CHUNKS, 16, 16, cw), BF16),
            pltpu.VMEM((CHUNKS, 2, 2, 4, 16, cw), BF16),
            pltpu.VMEM((CHUNKS, 2, 4, 16, cw), BF16),
            pltpu.VMEM((CHUNKS, 4, 16, cw), BF16),
            pltpu.VMEM((CHUNKS, 4, 16, cw), BF16),
            pltpu.VMEM((2, CHUNKS, 4, 16, cw), F32),
            pltpu.VMEM((CHUNKS, 2, 3, 16, cw), BF16),
            pltpu.VMEM((CHUNKS, 2, 3, 16, cw), BF16),
            pltpu.VMEM((CHUNKS, 2, 3, 16, cw), BF16),
            pltpu.VMEM((CHUNKS, 2, 3, 16, cw), BF16),
            pltpu.VMEM((KVH, 16, 128), BF16),
            pltpu.VMEM((16, 16, 128), BF16),
            pltpu.VMEM((tokens, 256), F32),
            pltpu.VMEM((tokens, columns), F32),
            pltpu.VMEM((tokens, 128), F32),
            pltpu.VMEM((tokens, 128), BF16),
            dma((5,)),
            dma((2, CHUNKS, 4)),
            dma((2, CHUNKS, 16)),
            dma((2, CHUNKS)),
            dma((16,)),
            dma((16,)),
            dma((CHUNKS,)),
            dma((CHUNKS,)),
            dma((CHUNKS,)),
            dma((CHUNKS,)),
            dma((CHUNKS, 2, 3)),
            dma((CHUNKS, 2, 3)),
            dma((CHUNKS, 2, 3)),
            dma((CHUNKS, 2, 3)),
        ],
        compiler_params=pltpu.CompilerParams(
            collective_id=0, has_side_effects=True, vmem_limit_bytes=56 * 1024 * 1024
        ),
        name="attention_block",
    )(
        hidden, positions.reshape(1, tokens), norm_in.reshape(1, features),
        norm_out.reshape(1, features), w_query, w_key.T, w_value.T, w_out, w_next,
    )


def fits(hidden, positions, w_query, w_key):
    return (
        lax.axis_size("tensor") == 16
        and hidden.shape[0] == 8
        and positions.shape[0] == 128
        and w_query.shape[1] == 128
        and w_key.shape[1] == 64
        and hidden.shape[1] % (2 * CHUNKS * 128) == 0
    )


def on_device(hidden, positions, norm_in, w_query, w_key, w_value, w_out, norm_out, w_next):
    if fits(hidden, positions, w_query, w_key):
        return fused(
            hidden, positions, norm_in, w_query, w_key, w_value, w_out, norm_out, w_next
        )
    width = lax.axis_size("tensor")
    tokens = positions.shape[0]
    share = hidden.shape[0]
    features = hidden.shape[1]
    head_dim = w_query.shape[1]
    key_cols = w_key.shape[1]
    residual = hidden.astype(jnp.float32)
    x_in = normalize(residual, norm_in).astype(jnp.bfloat16)
    w_input = jnp.concatenate([w_query, w_key, w_value], axis=1)
    projected = jnp.dot(
        lax.all_gather(x_in, "tensor", axis=0, tiled=True),
        w_input,
        preferred_element_type=jnp.float32,
    )
    queries = rotary(projected[:, :head_dim], positions, head_dim).astype(jnp.bfloat16)
    key_raw = projected[:, head_dim : head_dim + key_cols].astype(jnp.bfloat16)
    value_local = projected[:, head_dim + key_cols :].astype(jnp.bfloat16)
    local = jnp.stack([key_raw, value_local], axis=0).reshape(2, tokens, key_cols // KVH, KVH)
    per_group = jnp.transpose(local, (3, 0, 1, 2))
    sent = jnp.repeat(per_group, width // KVH, axis=0)
    pairs = lax.all_to_all(sent, "tensor", split_axis=0, concat_axis=0, tiled=True)
    pairs = jnp.transpose(pairs, (1, 2, 0, 3)).reshape(2, tokens, head_dim)
    key_block = rotary(pairs[0].astype(jnp.float32), positions, head_dim).astype(jnp.bfloat16)
    value_block = pairs[1]
    context = attend(queries, key_block, value_block, positions)
    packed = jnp.dot(context, w_out, preferred_element_type=jnp.float32).astype(jnp.bfloat16)
    received = lax.all_to_all(packed, "tensor", split_axis=0, concat_axis=0, tiled=True)
    mixed = jnp.sum(received.reshape(width, share, features).astype(jnp.float32), axis=0)
    residual_f = residual + mixed
    residual_out = residual_f.astype(jnp.bfloat16)
    x_next = normalize(residual_f, norm_out).astype(jnp.bfloat16)
    next_raw = jnp.dot(
        lax.all_gather(x_next, "tensor", axis=0, tiled=True),
        w_next,
        preferred_element_type=jnp.float32,
    )
    query_next = rotary(next_raw, positions, head_dim).astype(jnp.bfloat16)
    return (residual_out, query_next)


def solution(mesh):
    placed = (
        P(("groups", "tensor"), None),
        P("groups"),
        P(),
        P(None, "tensor"),
        P(None, "tensor"),
        P(None, "tensor"),
        P("tensor", None),
        P(),
        P(None, "tensor"),
    )
    return jax.shard_map(
        on_device,
        mesh=mesh,
        in_specs=placed,
        out_specs=(P(("groups", "tensor"), None), P("groups", "tensor")),
        check_vma=False,
    )
```

```python
import math

import jax
import jax.numpy as jnp
from jax import lax
from jax.experimental import pallas as pl
from jax.experimental.pallas import tpu as pltpu
from jax.sharding import PartitionSpec as P

KVH = 8
CHUNKS = 8
FIRST_Y = (7,)
NEXT_Y = (6, 7)
SUM_Z = (0, 1)
OWN, PRE, ALONG1, ALONG2, ALONG3, OVER0, OVER1, OVER2, OVER3, LAST = range(10)
MULT, SUMC, SUMA, HOP0, HOP1, HOP2, YFIN, FIN = range(10, 18)
ORDER_FIRST = (
    (OWN, 3), (OWN, 0), (OWN, 6), (OWN, 2), (OWN, 4), (OWN, 1), (ALONG1, 6), (OWN, 7), (OWN, 5),
    (ALONG1, 2), (ALONG1, 1), (ALONG1, 4), (OVER0, 2), (OVER0, 6), (ALONG2, 6), (PRE, 7), (ALONG1, 3),
    (OVER0, 4), (ALONG2, 2), (OVER0, 1), (ALONG2, 1), (OVER1, 6), (ALONG3, 6), (ALONG2, 4), (ALONG1, 5),
    (OVER0, 5), (OVER0, 3), (OVER1, 1), (ALONG1, 0), (OVER1, 2), (ALONG2, 3), (ALONG3, 2), (OVER0, 0),
    (OVER2, 6), (OVER3, 6), (OVER1, 4), (ALONG1, 7), (ALONG3, 1), (ALONG3, 4), (OVER1, 3), (ALONG2, 0),
    (OVER2, 1), (OVER2, 2), (ALONG2, 5), (ALONG2, 7), (OVER3, 2), (OVER2, 4), (ALONG3, 3), (OVER3, 1),
    (OVER3, 4), (OVER1, 5), (OVER1, 0), (ALONG3, 0), (LAST, 1), (ALONG3, 5), (LAST, 2), (OVER2, 3),
    (LAST, 4), (OVER3, 3), (LAST, 6), (OVER2, 0), (ALONG3, 7), (LAST, 3), (OVER3, 0), (OVER2, 5),
    (OVER3, 5), (LAST, 7), (LAST, 0), (LAST, 5),
)
ORDER_NEXT = (
    (MULT, 0), (MULT, 4), (MULT, 1), (SUMC, 0), (HOP0, 0), (SUMC, 4), (SUMC, 1), (MULT, 7), (MULT, 5),
    (MULT, 2), (SUMC, 2), (HOP0, 1), (MULT, 3), (HOP1, 0), (SUMC, 3), (HOP2, 0), (SUMC, 5), (SUMA, 4),
    (HOP1, 1), (HOP0, 4), (SUMA, 2), (MULT, 6), (HOP0, 2), (YFIN, 0), (HOP1, 4), (SUMC, 6), (HOP2, 1),
    (HOP1, 2), (SUMA, 3), (HOP0, 3), (SUMA, 5), (FIN, 0), (HOP2, 4), (OWN, 0), (YFIN, 1), (SUMC, 7),
    (HOP1, 3), (HOP2, 2), (HOP0, 5), (FIN, 4), (SUMA, 6), (HOP0, 6), (ALONG1, 0), (OWN, 4), (HOP1, 5),
    (FIN, 2), (OWN, 2), (HOP2, 3), (OVER0, 0), (ALONG2, 0), (FIN, 1), (HOP1, 6), (HOP2, 5), (SUMA, 7),
    (HOP0, 7), (OWN, 1), (FIN, 5), (OVER1, 0), (ALONG1, 4), (FIN, 3), (ALONG3, 0), (ALONG1, 2), (OWN, 3),
    (OVER2, 0), (HOP2, 6), (HOP1, 7), (OVER3, 0), (OWN, 5), (FIN, 6), (OWN, 6), (ALONG1, 1), (OVER0, 4),
    (HOP2, 7), (OVER0, 1), (OVER0, 2), (ALONG2, 2), (FIN, 7), (OWN, 7), (ALONG2, 4), (ALONG1, 3),
    (OVER1, 4), (PRE, 6), (ALONG1, 5), (ALONG2, 1), (LAST, 0), (OVER1, 1), (OVER0, 5), (ALONG3, 4),
    (OVER1, 2), (PRE, 7), (OVER0, 3), (ALONG2, 3), (OVER2, 4), (ALONG2, 5), (ALONG1, 6), (ALONG3, 1),
    (ALONG1, 7), (OVER1, 3), (ALONG3, 3), (OVER2, 1), (ALONG3, 2), (OVER1, 5), (OVER2, 2), (ALONG3, 5),
    (OVER3, 1), (ALONG2, 6), (OVER2, 5), (OVER2, 3), (OVER3, 3), (OVER3, 4), (OVER3, 2), (ALONG2, 7),
    (LAST, 3), (LAST, 1), (OVER3, 5), (ALONG3, 6), (LAST, 4), (LAST, 2), (LAST, 6), (ALONG3, 7), (LAST, 5),
    (LAST, 7),
)
F32 = jnp.float32
BF16 = jnp.bfloat16


def normalize(values, gain):
    mean_square = jnp.mean(values * values, axis=-1, keepdims=True)
    return values * lax.rsqrt(mean_square + 1e-05) * gain


def rotary(values, positions, head_dim):
    count = values.shape[0]
    heads_here = values.shape[1] // head_dim
    half = head_dim // 2
    shaped = values.reshape(count, heads_here, head_dim)
    inverse = jnp.exp(-math.log(500000.0) * (2.0 * jnp.arange(half, dtype=jnp.float32) / head_dim))
    angle = positions.astype(jnp.float32)[:, None] * inverse[None, :]
    cosine = jnp.cos(angle)[:, None, :]
    sine = jnp.sin(angle)[:, None, :]
    first = shaped[:, :, :half]
    second = shaped[:, :, half:]
    turned = jnp.concatenate(
        [first * cosine - second * sine, second * cosine + first * sine], axis=-1
    )
    return turned.reshape(count, heads_here * head_dim)


def attend(query, key_block, value_block, positions):
    count = positions.shape[0]
    order = jnp.arange(count, dtype=jnp.int32)
    allowed = (order[:, None] >= order[None, :]) & (
        positions[:, None] - positions[None, :] == order[:, None] - order[None, :]
    )
    scores = jnp.dot(query, key_block.T, preferred_element_type=jnp.float32) * (
        1.0 / math.sqrt(query.shape[1])
    )
    scores = jnp.where(allowed, scores, -1e30)
    largest = jnp.max(scores, axis=-1, keepdims=True)
    weights = jnp.where(allowed, jnp.exp(scores - largest), 0.0)
    weights = (weights / jnp.sum(weights, axis=-1, keepdims=True)).astype(jnp.bfloat16)
    return jnp.dot(weights, value_block, preferred_element_type=jnp.float32).astype(jnp.bfloat16)


def block_kernel(
    hid, pos, gain_in, gain_out, wq_hbm, wk_hbm, wv_hbm, wo_hbm, wn_hbm,
    res_out, next_out,
    wq, wkv, wo, wn, xg1, xg2, part, rb1, s1, rb2, s2, up_out, up_in, down_out, down_in,
    kvs, kvr, acc, acc_next, squares, ctx,
    w_sem, ag_send, ag_recv, sib_in, kv_send, kv_recv, sib_send, sib_recv, y_send, y_recv,
    up_send, up_recv, down_send, down_recv,
):
    me = lax.axis_index("tensor")
    c, y, z = lax.rem(me, 2), lax.rem(me // 2, 2), me // 4
    width = 16
    features = hid.shape[1]
    half = features // 2
    key_cols = wk_hbm.shape[0]
    nt = (((1,), (1,)), ((), ()))
    cw = half // CHUNKS
    tile = min(512, cw)
    tiles = cw // tile

    def index(zz, yy, cc):
        return (zz * 2 + yy) * 2 + cc

    sibling, across = index(z, y, 1 - c), index(z, 1 - y, c)
    upper, lower = index(z + 1, y, c), index(z - 1, y, c)
    pending = []

    def remote(src, dst, send, recv, device):
        return pltpu.make_async_remote_copy(
            src_ref=src, dst_ref=dst, send_sem=send, recv_sem=recv,
            device_id={"tensor": device}, device_id_type=pl.DeviceIdType.MESH,
        )

    def launch(make, when=None):
        if when is None:
            make().start()
        else:
            pl.when(when)(lambda: make().start())
        pending.append((make, when))

    weights = [
        pltpu.make_async_copy(src, dst, w_sem.at[i])
        for i, (src, dst) in enumerate(
            [(wq_hbm, wq), (wk_hbm, wkv.at[:key_cols]), (wv_hbm, wkv.at[key_cols:]), (wo_hbm, wo), (wn_hbm, wn)]
        )
    ]
    for copy in weights:
        copy.start()

    barrier = pltpu.get_barrier_semaphore()

    def greet(device):
        pl.semaphore_signal(
            barrier, inc=1, device_id={"tensor": device}, device_id_type=pl.DeviceIdType.MESH
        )

    greet(sibling)
    greet(across)
    pl.when(z < 3)(lambda: greet(upper))
    pl.when(z > 0)(lambda: greet(lower))

    def hidden_rows(k, off, size):
        first = hid[:, pl.ds(k * cw + off, size)].astype(F32)
        second = hid[:, pl.ds(half + k * cw + off, size)].astype(F32)
        return jnp.concatenate([first, second], axis=0)

    for k in range(CHUNKS):
        xg1[k, me] = hidden_rows(k, 0, cw).astype(BF16)
    acc[...] = jnp.zeros_like(acc)
    acc_next[...] = jnp.zeros_like(acc_next)
    squares[...] = jnp.zeros_like(squares)
    inner = (z > 0) & (z < 3)
    pl.when(inner)(lambda: pl.semaphore_wait(barrier, 4))
    pl.when(jnp.logical_not(inner))(lambda: pl.semaphore_wait(barrier, 3))

    def gather_stages(a, xg, y_first):
        def copy(k, origin, way, device):
            arrival = sib_in.at[a, k] if way == 3 else ag_recv.at[a, k, origin]
            return remote(
                xg.at[k, origin], xg.at[k, origin], ag_send.at[a, k, way], arrival, device
            )

        def blocks(k, count, way):
            return remote(
                xg.at[k, pl.ds(0, count)], xg.at[k, pl.ds(0, count)],
                ag_send.at[a, k, way], sib_in.at[a, k], sibling,
            )

        def arrived(k, origin):
            copy(k, origin, 0, sibling).wait_recv()

        def own(k):
            copy(k, me, 2, across).start()
            pl.when(z < 3)(lambda: copy(k, me, 0, upper).start())
            pl.when(z > 0)(lambda: copy(k, me, 1, lower).start())
            copy(k, me, 3, sibling).start()

        def early(k):
            if k in y_first:
                origin = index(z, 1 - y, c)
                arrived(k, origin)
                pl.when(z < 3)(lambda: copy(k, origin, 0, upper).start())
                pl.when(z > 0)(lambda: copy(k, origin, 1, lower).start())
                copy(k, origin, 3, sibling).start()

        def along(d):
            def both(k):
                for yy in (y, 1 - y):
                    @pl.when(z >= d)
                    def _(origin=index(z - d, yy, c)):
                        arrived(k, origin)
                        if d < 3:
                            pl.when(z < 3)(lambda: copy(k, origin, 0, upper).start())
                        copy(k, origin, 3, sibling).start()

                    @pl.when(z + d <= 3)
                    def _(origin=index(z + d, yy, c)):
                        arrived(k, origin)
                        if d < 3:
                            pl.when(z > 0)(lambda: copy(k, origin, 1, lower).start())
                        copy(k, origin, 3, sibling).start()

            def stage(k):
                if k in y_first:
                    both(k)
                    return

                @pl.when(z >= d)
                def _():
                    origin = index(z - d, y, c)
                    arrived(k, origin)
                    copy(k, origin, 2, across).start()
                    if d < 3:
                        pl.when(z < 3)(lambda: copy(k, origin, 0, upper).start())
                    copy(k, origin, 3, sibling).start()

                @pl.when(z + d <= 3)
                def _():
                    origin = index(z + d, y, c)
                    arrived(k, origin)
                    copy(k, origin, 2, across).start()
                    if d < 3:
                        pl.when(z > 0)(lambda: copy(k, origin, 1, lower).start())
                    copy(k, origin, 3, sibling).start()
            return stage

        def over(d):
            def pass_on(k, zz):
                origin = index(zz, 1 - y, c)
                arrived(k, origin)
                copy(k, origin, 3, sibling).start()

            def stage(k):
                if k in y_first:
                    return
                if d == 0:
                    pass_on(k, z)
                else:
                    pl.when(z >= d)(lambda: pass_on(k, z - d))
                    pl.when(z + d <= 3)(lambda: pass_on(k, z + d))
            return stage

        def last(k):
            blocks(k, 8, 3).wait_recv()

        def sent(k):
            spread = 2 if k in y_first else 1
            blocks(k, 1 if k in y_first else 4, 2).wait_send()
            blocks(k, 8, 3).wait_send()
            for at in range(4):
                @pl.when(z == at)
                def _(at=at):
                    if at < 3:
                        blocks(k, spread * (at + 1), 0).wait_send()
                    if at > 0:
                        blocks(k, spread * (4 - at), 1).wait_send()

        return own, early, along, over, last, sent

    def run(stages, order):
        for name, k in order:
            stages[name](k)

    def consume(xg, gain, add, k):
        @pl.loop(0, tiles)
        def _(j):
            off = pl.multiple_of(j * tile, tile)
            block = xg[k, :, :, pl.ds(off, tile)].astype(F32)
            part_sq = squares[...]
            for h in (0, 1):
                rows = block[:, 8 * h : 8 * h + 8, :].reshape(8 * width, tile)
                for i in range(tile // 128):
                    piece = rows[:, 128 * i : 128 * (i + 1)]
                    part_sq = part_sq + piece * piece
                at = pl.multiple_of(h * half + k * cw + off, tile)
                scaled = (rows * gain[:, pl.ds(at, tile)]).astype(BF16)
                add(scaled, pl.ds(at, tile))
            squares[...] = part_sq

    def inverse_norm():
        mean_square = jnp.sum(squares[...], axis=1, keepdims=True) * (1.0 / features)
        return lax.rsqrt(mean_square + 1e-05)

    own, early, along, over, last, sent = gather_stages(0, xg1, FIRST_Y)

    def add_projections(scaled, at):
        acc[:, :128] += jnp.dot(scaled, wq[at, :], preferred_element_type=F32)
        acc[:, 128:] += lax.dot_general(scaled, wkv[:, at], nt, preferred_element_type=F32)

    first_used = [k for name, k in ORDER_FIRST if name == LAST][0]

    def project(k):
        if k == first_used:
            for copy in weights[:3]:
                copy.wait()
        last(k)
        consume(xg1, gain_in, add_projections, k)

    run({OWN: own, PRE: early, ALONG1: along(1), ALONG2: along(2), ALONG3: along(3), OVER0: over(0),
         OVER1: over(1), OVER2: over(2), OVER3: over(3), LAST: project}, ORDER_FIRST)

    scale = inverse_norm()
    squares[...] = jnp.zeros_like(squares)
    raw = acc[...] * scale
    queries = raw[:, :128]
    kv = raw[:, 128:].astype(BF16)
    out_row = lax.broadcasted_iota(jnp.int32, (128, 128), 0)
    in_col = lax.broadcasted_iota(jnp.int32, (128, 128), 1)
    wanted = ((out_row // 8) % 2) * 64 + (out_row % 8) * 8 + out_row // 16
    order = jnp.where(in_col == wanted, 1.0, 0.0).astype(BF16)
    turned = lax.dot_general(order, kv, nt, preferred_element_type=F32)
    kvs[...] = turned.astype(BF16).reshape(KVH, 16, 128)

    def kv_copy(step):
        peer = lax.rem(me + step, width)
        return lambda: remote(
            kvs.at[peer // 2], kvr.at[me], kv_send.at[step], kv_recv.at[me], peer
        )

    for step in range(1, width):
        launch(kv_copy(step))
    kvr[me] = kvs[me // 2]

    for k in range(CHUNKS):
        sent(k)

    token_pos = jnp.broadcast_to(pos[...].astype(F32), (128, 128))
    exponent = lax.broadcasted_iota(jnp.int32, (64, 128), 0).astype(F32)
    inverse = jnp.exp(-math.log(500000.0) * (2.0 * exponent / 128))
    angle = token_pos[:64] * inverse
    cos_t, sin_t = jnp.cos(angle), jnp.sin(angle)
    cosine = jnp.concatenate([cos_t, cos_t], axis=0).T
    sine = jnp.concatenate([-sin_t, sin_t], axis=0).T

    def turn(values):
        return values * cosine + pltpu.roll(values, 64, 1) * sine

    query = turn(queries).astype(BF16)
    row = lax.broadcasted_iota(jnp.int32, (128, 128), 0).astype(F32)
    col = lax.broadcasted_iota(jnp.int32, (128, 128), 1).astype(F32)
    allowed = (row >= col) & (token_pos.T - token_pos == row - col)

    for step in range(1, width):
        source = lax.rem(me + step, width)
        remote(kvs.at[0], kvr.at[source], kv_send.at[step], kv_recv.at[source], sibling).wait_recv()
    both = kvr[...].astype(F32)
    key_t = both[:, 0:8, :].reshape(128, 128)
    value_t = both[:, 8:16, :].reshape(128, 128).astype(BF16)
    first, second = key_t[:64], key_t[64:]
    key_rows = jnp.concatenate(
        [first * cos_t - second * sin_t, second * cos_t + first * sin_t], axis=0
    ).astype(BF16)
    scores = jnp.dot(query, key_rows, preferred_element_type=F32) * (1.0 / math.sqrt(128))
    scores = jnp.where(allowed, scores, -1e30)
    largest = jnp.max(scores, axis=-1, keepdims=True)
    attn = jnp.where(allowed, jnp.exp(scores - largest), 0.0)
    attn = (attn / jnp.sum(attn, axis=-1, keepdims=True)).astype(BF16)
    ctx[...] = lax.dot_general(attn, value_t, nt, preferred_element_type=F32).astype(BF16)

    def tiled(body):
        @pl.loop(0, tiles)
        def _(j):
            body(pl.multiple_of(j * tile, tile))

    def multiply(k):
        if k == ORDER_NEXT[0][1]:
            weights[3].wait()

        def body(off):
            at = pl.multiple_of(k * cw + off, tile)
            one = jnp.dot(ctx[...], wo[:, pl.ds(at, tile)], preferred_element_type=F32)
            at = pl.multiple_of(half + k * cw + off, tile)
            two = jnp.dot(ctx[...], wo[:, pl.ds(at, tile)], preferred_element_type=F32)
            for t in range(width):
                rows = jnp.concatenate([one[8 * t : 8 * t + 8], two[8 * t : 8 * t + 8]], axis=0)
                part[k, t % 2, (t // 2) % 2, t // 4, :, pl.ds(off, tile)] = rows.astype(BF16)

        tiled(body)
        launch(lambda: remote(part.at[k, 1 - c], rb1.at[k], sib_send.at[k], sib_recv.at[k], sibling))

    def sum_cores(k):
        remote(part.at[k, 1 - c], rb1.at[k], sib_send.at[k], sib_recv.at[k], sibling).wait_recv()

        def body(off):
            cols = pl.ds(off, tile)
            theirs = (
                part[k, c, 1 - y, :, :, cols].astype(F32) + rb1[k, 1 - y, :, :, cols].astype(F32)
            )
            if k in SUM_Z:
                s2[1, k, :, :, cols] = theirs
                s2[0, k, :, :, cols] = (
                    part[k, c, y, :, :, cols].astype(F32) + rb1[k, y, :, :, cols].astype(F32)
                )
            else:
                s1[k, :, :, cols] = theirs.astype(BF16)

        tiled(body)
        if k in SUM_Z:
            return
        launch(lambda: remote(s1.at[k], rb2.at[k], y_send.at[k], y_recv.at[k], across))

    def sum_across(k):
        if k in SUM_Z:
            return
        remote(s1.at[k], rb2.at[k], y_send.at[k], y_recv.at[k], across).wait_recv()

        def body(off):
            cols = pl.ds(off, tile)
            s2[0, k, :, :, cols] = (
                part[k, c, y, :, :, cols].astype(F32)
                + rb1[k, y, :, :, cols].astype(F32)
                + rb2[k, :, :, cols].astype(F32)
            )

        tiled(body)

    def up_copy(k, o, target):
        i = target - 1
        return lambda: remote(
            up_out.at[k, o, i], up_in.at[k, o, i], up_send.at[k, o, i], up_recv.at[k, o, i], upper
        )

    def down_copy(k, o, target):
        return lambda: remote(
            down_out.at[k, o, target], down_in.at[k, o, target], down_send.at[k, o, target],
            down_recv.at[k, o, target], lower,
        )

    def hop(j):
        def stage(k):
            for o in (0, 1) if k in SUM_Z else (0,):
                @pl.when(z == j)
                def _(o=o):
                    for target in range(3, j, -1):
                        value = s2[o, k, target]
                        if j > 0:
                            up_copy(k, o, target)().wait_recv()
                            value = value + up_in[k, o, target - 1].astype(F32)
                        up_out[k, o, target - 1] = value.astype(BF16)
                        up_copy(k, o, target)().start()

                @pl.when(z == 3 - j)
                def _(o=o):
                    for target in range(3 - j):
                        value = s2[o, k, target]
                        if j > 0:
                            down_copy(k, o, target)().wait_recv()
                            value = value + down_in[k, o, target].astype(F32)
                        down_out[k, o, target] = value.astype(BF16)
                        down_copy(k, o, target)().start()

                for target in range(3, j, -1):
                    pending.append((up_copy(k, o, target), z == j))
                for target in range(3 - j):
                    pending.append((down_copy(k, o, target), z == 3 - j))
        return stage

    def whole_line(k, o, then):
        for target in range(4):
            @pl.when(z == target)
            def _(target=target):
                value = s2[o, k, target]
                if target > 0:
                    up_copy(k, o, target)().wait_recv()
                    value = value + up_in[k, o, target - 1].astype(F32)
                if target < 3:
                    down_copy(k, o, target)().wait_recv()
                    value = value + down_in[k, o, target].astype(F32)
                then(value)

    def across_copy(k):
        return lambda: remote(s1.at[k, 0], rb2.at[k, 0], y_send.at[k], y_recv.at[k], across)

    def hand_across(k):
        if k in SUM_Z:
            def keep(value):
                s1[k, 0] = value.astype(BF16)
            whole_line(k, 1, keep)
            launch(across_copy(k))

    def drain():
        for make, when in pending:
            if when is None:
                make().wait_send()
            else:
                pl.when(when)(lambda make=make: make().wait_send())

    own2, early2, along2, over2, last2, sent2 = gather_stages(1, xg2, NEXT_Y)

    def finish(k):
        def keep(value):
            s2[0, k, 0] = value
        whole_line(k, 0, keep)
        mixed = s2[0, k, 0]
        if k in SUM_Z:
            across_copy(k)().wait_recv()
            mixed = mixed + rb2[k, 0].astype(F32)
        residual = mixed + hidden_rows(k, 0, cw)
        res_out[:, pl.ds(k * cw, cw)] = residual[:8].astype(BF16)
        res_out[:, pl.ds(half + k * cw, cw)] = residual[8:].astype(BF16)
        xg2[k, me] = residual.astype(BF16)

    def add_next(scaled, at):
        acc_next[...] += jnp.dot(scaled, wn[at, :], preferred_element_type=F32)

    next_used = [k for name, k in ORDER_NEXT if name == LAST][0]

    def project_next(k):
        if k == next_used:
            weights[4].wait()
        if k == ORDER_NEXT[-1][1]:
            drain()
        last2(k)
        consume(xg2, gain_out, add_next, k)

    run({MULT: multiply, SUMC: sum_cores, SUMA: sum_across, HOP0: hop(0), HOP1: hop(1), HOP2: hop(2),
         YFIN: hand_across, FIN: finish, OWN: own2, PRE: early2, ALONG1: along2(1), ALONG2: along2(2),
         ALONG3: along2(3), OVER0: over2(0), OVER1: over2(1), OVER2: over2(2), OVER3: over2(3),
         LAST: project_next}, ORDER_NEXT)

    next_out[...] = turn(acc_next[...] * inverse_norm()).astype(BF16)

    for k in range(CHUNKS):
        sent2(k)


def fused(hidden, positions, norm_in, w_query, w_key, w_value, w_out, norm_out, w_next):
    share, features = hidden.shape
    tokens = positions.shape[0]
    cw = features // 2 // CHUNKS
    columns = w_query.shape[1]
    vmem = pl.BlockSpec(memory_space=pltpu.VMEM)
    anywhere = pl.BlockSpec(memory_space=pl.ANY)
    dma = pltpu.SemaphoreType.DMA
    return pl.pallas_call(
        block_kernel,
        out_shape=(
            jax.ShapeDtypeStruct((share, features), BF16),
            jax.ShapeDtypeStruct((tokens, columns), BF16),
        ),
        in_specs=[vmem] * 4 + [anywhere] * 5,
        out_specs=(vmem, vmem),
        scratch_shapes=[
            pltpu.VMEM(w_query.shape, BF16),
            pltpu.VMEM((2 * w_key.shape[1], features), BF16),
            pltpu.VMEM(w_out.shape, BF16),
            pltpu.VMEM(w_next.shape, BF16),
            pltpu.VMEM((CHUNKS, 16, 16, cw), BF16),
            pltpu.VMEM((CHUNKS, 16, 16, cw), BF16),
            pltpu.VMEM((CHUNKS, 2, 2, 4, 16, cw), BF16),
            pltpu.VMEM((CHUNKS, 2, 4, 16, cw), BF16),
            pltpu.VMEM((CHUNKS, 4, 16, cw), BF16),
            pltpu.VMEM((CHUNKS, 4, 16, cw), BF16),
            pltpu.VMEM((2, CHUNKS, 4, 16, cw), F32),
            pltpu.VMEM((CHUNKS, 2, 3, 16, cw), BF16),
            pltpu.VMEM((CHUNKS, 2, 3, 16, cw), BF16),
            pltpu.VMEM((CHUNKS, 2, 3, 16, cw), BF16),
            pltpu.VMEM((CHUNKS, 2, 3, 16, cw), BF16),
            pltpu.VMEM((KVH, 16, 128), BF16),
            pltpu.VMEM((16, 16, 128), BF16),
            pltpu.VMEM((tokens, 256), F32),
            pltpu.VMEM((tokens, columns), F32),
            pltpu.VMEM((tokens, 128), F32),
            pltpu.VMEM((tokens, 128), BF16),
            dma((5,)),
            dma((2, CHUNKS, 4)),
            dma((2, CHUNKS, 16)),
            dma((2, CHUNKS)),
            dma((16,)),
            dma((16,)),
            dma((CHUNKS,)),
            dma((CHUNKS,)),
            dma((CHUNKS,)),
            dma((CHUNKS,)),
            dma((CHUNKS, 2, 3)),
            dma((CHUNKS, 2, 3)),
            dma((CHUNKS, 2, 3)),
            dma((CHUNKS, 2, 3)),
        ],
        compiler_params=pltpu.CompilerParams(
            collective_id=0, has_side_effects=True, vmem_limit_bytes=56 * 1024 * 1024
        ),
        name="attention_block",
    )(
        hidden, positions.reshape(1, tokens), norm_in.reshape(1, features),
        norm_out.reshape(1, features), w_query, w_key.T, w_value.T, w_out, w_next,
    )


def fits(hidden, positions, w_query, w_key):
    return (
        lax.axis_size("tensor") == 16
        and hidden.shape[0] == 8
        and positions.shape[0] == 128
        and w_query.shape[1] == 128
        and w_key.shape[1] == 64
        and hidden.shape[1] % (2 * CHUNKS * 128) == 0
    )


def on_device(hidden, positions, norm_in, w_query, w_key, w_value, w_out, norm_out, w_next):
    if fits(hidden, positions, w_query, w_key):
        return fused(
            hidden, positions, norm_in, w_query, w_key, w_value, w_out, norm_out, w_next
        )
    width = lax.axis_size("tensor")
    tokens = positions.shape[0]
    share = hidden.shape[0]
    features = hidden.shape[1]
    head_dim = w_query.shape[1]
    key_cols = w_key.shape[1]
    residual = hidden.astype(jnp.float32)
    x_in = normalize(residual, norm_in).astype(jnp.bfloat16)
    w_input = jnp.concatenate([w_query, w_key, w_value], axis=1)
    projected = jnp.dot(
        lax.all_gather(x_in, "tensor", axis=0, tiled=True),
        w_input,
        preferred_element_type=jnp.float32,
    )
    queries = rotary(projected[:, :head_dim], positions, head_dim).astype(jnp.bfloat16)
    key_raw = projected[:, head_dim : head_dim + key_cols].astype(jnp.bfloat16)
    value_local = projected[:, head_dim + key_cols :].astype(jnp.bfloat16)
    local = jnp.stack([key_raw, value_local], axis=0).reshape(2, tokens, key_cols // KVH, KVH)
    per_group = jnp.transpose(local, (3, 0, 1, 2))
    sent = jnp.repeat(per_group, width // KVH, axis=0)
    pairs = lax.all_to_all(sent, "tensor", split_axis=0, concat_axis=0, tiled=True)
    pairs = jnp.transpose(pairs, (1, 2, 0, 3)).reshape(2, tokens, head_dim)
    key_block = rotary(pairs[0].astype(jnp.float32), positions, head_dim).astype(jnp.bfloat16)
    value_block = pairs[1]
    context = attend(queries, key_block, value_block, positions)
    packed = jnp.dot(context, w_out, preferred_element_type=jnp.float32).astype(jnp.bfloat16)
    received = lax.all_to_all(packed, "tensor", split_axis=0, concat_axis=0, tiled=True)
    mixed = jnp.sum(received.reshape(width, share, features).astype(jnp.float32), axis=0)
    residual_f = residual + mixed
    residual_out = residual_f.astype(jnp.bfloat16)
    x_next = normalize(residual_f, norm_out).astype(jnp.bfloat16)
    next_raw = jnp.dot(
        lax.all_gather(x_next, "tensor", axis=0, tiled=True),
        w_next,
        preferred_element_type=jnp.float32,
    )
    query_next = rotary(next_raw, positions, head_dim).astype(jnp.bfloat16)
    return (residual_out, query_next)


def solution(mesh):
    placed = (
        P(("groups", "tensor"), None),
        P("groups"),
        P(),
        P(None, "tensor"),
        P(None, "tensor"),
        P(None, "tensor"),
        P("tensor", None),
        P(),
        P(None, "tensor"),
    )
    return jax.shard_map(
        on_device,
        mesh=mesh,
        in_specs=placed,
        out_specs=(P(("groups", "tensor"), None), P("groups", "tensor")),
        check_vma=False,
    )
```
